256 devices in a mesh: tm: 8 (over x, y_lo), height: 32 (over z, y_hi, core).
Axes of the slice: x: 4, y: 4 (y_hi: 2, y_lo: 2; y = y_hi * 2 + y_lo), z: 8, core: 2. Of those that a mesh axis runs over, the one named last changes fastest.
Arguments:
- latent: bfloat16 [8, 64, 104, 1536], P('tm', 'height'), may hold values from -6 to 6
- modulation: float32 [3, 1536], replicated, may hold values from -3 to 3
- cross_norm: float32 [2, 1536], replicated, may hold values from -1.5 to 1.5
- norm_gains: float32 [4, 768], replicated, may hold values from 0.5 to 8
- w_main: bfloat16 [1536, 4608], P('height'), may hold values from -0.14505926 to 0.14505926
- text_states: bfloat16 [512, 1536], replicated, may hold values from -6 to 6
- w_text: bfloat16 [1536, 1536], P(None, 'height'), may hold values from -0.10257238 to 0.10257238
- tile_offsets: int32 [3, 8, 32, 4, 8], P(None, 'tm', 'height'), may hold values from -1 to 1, as said below
- text_mask: int32 [512], replicated, may hold values from 0 to 1
Outputs:
- block_out: bfloat16 [8, 64, 104, 1536], P('tm', 'height')
The draws below stay inside these ranges and needn't reach their ends.
Inputs may be any that keep to these rules, and one draw needn't show every extreme that they name: `tile_offsets`: for each query tile the 8 offsets are distinct and none is (0, 0, 0).
All inputs are finite; a program needn't handle non-finite values.
Results may differ from the reference program's by a relative error of at most 0.0065.
Values may be sent and summed in bfloat16 or wider, within the bound.
A program may use at most 128 MiB of HBM per device.

```python
import jax
import jax.numpy as jnp
from jax import lax

D = 1536
HD = 128
TEXT = 512
HEADS = 6
W = 104
TH = 2
TW = 26
NB = 8
FRAMES = 8
H = 64
TILES_H = 32
TILES_W = 4


def inner_normal(key):
    head_width = HEADS * HD
    inner_key = jax.random.fold_in(key, 101)
    return jnp.clip(jax.random.normal(inner_key, (D, 4 * head_width), jnp.float32), -4.0, 4.0) * D ** (-0.5)


def draw_modulation(key, part):
    shift_key, scale_key, sign_key, gate_key = jax.random.split(key, 4)
    shift_row = jnp.clip(0.5 * jax.random.normal(shift_key, (D,), jnp.float32), -1.0, 1.0)
    scale_row = jnp.clip(0.4 * jax.random.normal(scale_key, (D,), jnp.float32), -0.8, 0.8)
    sign_row = jnp.where(jax.random.uniform(sign_key, (D,), jnp.float32) < 0.5, -1.0, 1.0)
    gate_row = sign_row * jax.random.uniform(gate_key, (D,), jnp.float32, 1.0, 3.0)
    return jnp.stack([shift_row, scale_row, gate_row]).astype(jnp.float32)


def draw_cross_norm(key, part):
    gain_key = jax.random.fold_in(key, 105)
    gain_row = jax.random.uniform(gain_key, (D,), jnp.float32, 0.5, 1.5)
    bias_row = jnp.clip(0.3 * jax.random.normal(jax.random.fold_in(key, 106), (D,), jnp.float32), -1.0, 1.0)
    return jnp.stack([gain_row, bias_row]).astype(jnp.float32)


def draw_norm_gains(key, part):
    head_width = HEADS * HD
    exponent = jax.random.uniform(key, (4, head_width), jnp.float32, jnp.log(0.5), jnp.log(2.5))
    return jnp.exp(exponent).astype(jnp.float32)


def draw_w_main(key, part):
    head_width = HEADS * HD
    outer_key = jax.random.fold_in(key, 102)
    inner = inner_normal(key)
    outer = jnp.clip(jax.random.normal(outer_key, (D, 2 * head_width), jnp.float32), -4.0, 4.0) * head_width ** (-0.5)
    return jnp.concatenate([inner, outer], axis=1).astype(jnp.bfloat16)


def draw_w_text(key, part):
    head_width = HEADS * HD
    both = jnp.clip(jax.random.normal(jax.random.fold_in(key, 103), (D, 2 * head_width), jnp.float32), -4.0, 4.0) * D ** (-0.5)
    return both.astype(jnp.bfloat16)


def draw_text_states(key, part):
    base_key = jax.random.fold_in(key, 108)
    rows_out = jnp.clip(jax.random.normal(base_key, (TEXT, D), jnp.float32), -6.0, 6.0)
    return rows_out.astype(jnp.bfloat16)


def draw_tile_offsets(key, part):
    tile_total = FRAMES * TILES_H * TILES_W
    rank_set = jax.random.randint(key, (tile_total, 26), 0, 1 << 20) * 32 + jnp.arange(26, dtype=jnp.int32)
    chosen = jnp.argsort(rank_set, axis=1)[:, :NB].astype(jnp.int32)
    code_set = chosen + (chosen >= 13).astype(jnp.int32)
    frame_step = code_set // 9 - 1
    row_step = code_set // 3 % 3 - 1
    col_step = code_set % 3 - 1
    return jnp.stack([frame_step, row_step, col_step]).reshape(3, FRAMES, TILES_H, TILES_W, NB).astype(jnp.int32)


def draw_text_mask(key, part):
    levels = jax.random.randint(key, (TEXT,), 0, 4)
    ones_at = (levels > 0).astype(jnp.int32)
    return jnp.where(jnp.arange(TEXT) == 0, 1, ones_at).astype(jnp.int32)


def block_scale(key, extent, shards, low, top_value):
    level = 1.0
    for dim, blocks in shards:
        steps = jax.random.uniform(jax.random.fold_in(jax.random.fold_in(key, 6), dim), (blocks,), jnp.float32, low / len(shards), top_value / len(shards))
        level = level * jnp.repeat(jnp.exp(steps), extent[dim] // blocks).reshape((-1,) + (1,) * (len(extent) - 1 - dim))
    return level


def normal_values(own_key, shape, deviation, limit, shards=(), kind=jnp.bfloat16):
    loudness = block_scale(own_key, shape, shards, -0.22, 0.18) if shards else 1.0
    entries = jax.random.normal(own_key, shape, jnp.float32) * deviation * loudness
    return jnp.minimum(jnp.maximum(entries, -limit), limit).astype(kind)


def setup_inputs(seed: int = 0) -> dict:
    key_list = jax.random.split(jax.random.key(seed), 10)
    latent = normal_values(key_list[0], (FRAMES, H, W, D), 1.0, 6.0, ((0, 8), (1, 32)))
    modulation = draw_modulation(jax.random.fold_in(key_list[9], 71), 0)
    cross_norm = draw_cross_norm(jax.random.fold_in(key_list[9], 71), 0)
    norm_gains = draw_norm_gains(jax.random.fold_in(key_list[9], 71), 0)
    w_main = draw_w_main(jax.random.fold_in(key_list[9], 71), 0)
    text_states = draw_text_states(jax.random.fold_in(key_list[9], 71), 0)
    w_text = draw_w_text(jax.random.fold_in(key_list[9], 71), 0)
    tile_offsets = draw_tile_offsets(jax.random.fold_in(key_list[9], 71), 0)
    text_mask = draw_text_mask(jax.random.fold_in(key_list[9], 71), 0)
    return {"latent": latent, "modulation": modulation, "cross_norm": cross_norm, "norm_gains": norm_gains, "w_main": w_main, "text_states": text_states, "w_text": w_text, "tile_offsets": tile_offsets, "text_mask": text_mask}


def layer_norm(values):
    average = lax.optimization_barrier(jnp.mean(values, axis=-1, keepdims=True))
    centred = values - average
    variance = lax.optimization_barrier(jnp.mean(centred * centred, axis=-1, keepdims=True))
    return centred * lax.rsqrt(variance + 1e-06)

def rms_norm(values, gain_vec):
    mean_square = lax.optimization_barrier(jnp.mean(values * values, axis=-1, keepdims=True))
    return values * lax.rsqrt(mean_square + 1e-06) * gain_vec

def to_tiles(field_in, tile_height, tile_width):
    frame_count, row_count, col_count, channels = field_in.shape
    shaped = field_in.reshape(frame_count, row_count // tile_height, tile_height, col_count // tile_width, tile_width, channels)
    shaped = shaped.transpose(0, 1, 3, 2, 4, 5)
    return shaped.reshape(frame_count, row_count // tile_height, col_count // tile_width, tile_height * tile_width, channels)

def from_tiles(tile_set, tile_height, tile_width):
    tile_rows, tile_cols, cell_count, channels = tile_set.shape
    shaped = tile_set.reshape(tile_rows, tile_cols, tile_height, tile_width, channels)
    shaped = shaped.transpose(0, 2, 1, 3, 4)
    return shaped.reshape(tile_rows * tile_height * tile_cols * tile_width, channels)

def neighbour_index(offsets, row_base, frame_at, frame_total, row_total, tile_rows, tile_cols):
    own_step = jnp.zeros((3, tile_rows, tile_cols, 1), jnp.int32)
    step_set = jnp.concatenate([own_step, offsets.astype(jnp.int32)], axis=3)
    frame_step = step_set[0]
    row_step = step_set[1]
    col_step = step_set[2]
    row_ids = lax.broadcasted_iota(jnp.int32, (tile_rows, tile_cols, 1), 0)
    col_ids = lax.broadcasted_iota(jnp.int32, (tile_rows, tile_cols, 1), 1)
    frame_to = frame_at + frame_step
    row_to = row_base + row_ids + row_step
    col_to = col_ids + col_step
    usable = (frame_to >= 0) & (frame_to < frame_total) & (row_to >= 0) & (row_to < row_total)
    usable = usable & (col_to >= 0) & (col_to < tile_cols)
    position = ((1 + frame_step) * (tile_rows + 2) + row_ids + 1 + row_step) * tile_cols + jnp.clip(col_to, 0, tile_cols - 1)
    return (position.reshape(-1).astype(jnp.int32), usable.reshape(tile_rows * tile_cols, -1))

def tile_attention(query_tiles, key_ext, value_ext, offsets, row_base, frame_at, frame_total, row_total):
    tile_rows, tile_cols, cell_count, head_width = query_tiles.shape
    head_channels = head_width // HEADS
    tile_count = tile_rows * tile_cols
    position, usable = neighbour_index(offsets, row_base, frame_at, frame_total, row_total, tile_rows, tile_cols)
    key_matrix = jnp.take(key_ext.reshape(-1, cell_count, head_width), position, axis=0).reshape(tile_count, -1, HEADS, head_channels)
    value_matrix = jnp.take(value_ext.reshape(-1, cell_count, head_width), position, axis=0).reshape(tile_count, -1, HEADS, head_channels)
    query_matrix = query_tiles.reshape(tile_count, cell_count, HEADS, head_channels)
    key_mask = jnp.repeat(usable, cell_count, axis=1)
    logit_scores = jnp.einsum('tphd,tkhd->thpk', query_matrix.astype(jnp.float32), key_matrix.astype(jnp.float32)) * head_channels ** (-0.5)
    logit_scores = jnp.where(key_mask[:, None, None, :], logit_scores, -jnp.inf)
    largest = lax.optimization_barrier(jnp.max(logit_scores, axis=-1, keepdims=True))
    exponent = jnp.exp(logit_scores - largest)
    attention_probs = (exponent / lax.optimization_barrier(jnp.sum(exponent, axis=-1, keepdims=True))).astype(jnp.bfloat16)
    blended_output = jnp.einsum('thpk,tkhd->tphd', attention_probs.astype(jnp.float32), value_matrix.astype(jnp.float32))
    return blended_output.astype(jnp.bfloat16).reshape(tile_rows, tile_cols, cell_count, head_width)

def cross_attention(query_flat, text_key_set, text_value_set, text_mask):
    token_count, head_width = query_flat.shape
    head_channels = head_width // HEADS
    query_matrix = query_flat.reshape(token_count, HEADS, head_channels).astype(jnp.float32)
    key_matrix = text_key_set.reshape(-1, HEADS, head_channels).astype(jnp.float32)
    logit_scores = jnp.einsum('jcb,ycb->cjy', query_matrix, key_matrix) * head_channels ** (-0.5)
    logit_scores = jnp.where((text_mask == 1)[None, None, :], logit_scores, -jnp.inf)
    largest = lax.optimization_barrier(jnp.max(logit_scores, axis=-1, keepdims=True))
    exponent = jnp.exp(logit_scores - largest)
    attention_probs = (exponent / lax.optimization_barrier(jnp.sum(exponent, axis=-1, keepdims=True))).astype(jnp.bfloat16)
    value_matrix = text_value_set.reshape(-1, HEADS, head_channels).astype(jnp.float32)
    blended_output = jnp.einsum('tgp,ptr->gtr', attention_probs.astype(jnp.float32), value_matrix)
    return blended_output.astype(jnp.bfloat16).reshape(token_count, head_width)

def reference(latent, modulation, cross_norm, norm_gains, w_main, text_states, w_text, tile_offsets, text_mask):
    frame_count, row_count, col_count, model_dim = latent.shape
    head_width = HEADS * HD

    def project(frame_in):
        flattened = frame_in.reshape(-1, model_dim).astype(jnp.float32)
        modulated = (layer_norm(flattened) * (1.0 + modulation[1]) + modulation[0]).astype(jnp.bfloat16)
        joined = jnp.dot(modulated, w_main[:, :3 * head_width], preferred_element_type=jnp.float32)
        query_out = rms_norm(joined[:, :head_width], norm_gains[0]).astype(jnp.bfloat16)
        key_out = rms_norm(joined[:, head_width:2 * head_width], norm_gains[1]).astype(jnp.bfloat16)
        value_out = joined[:, 2 * head_width:].astype(jnp.bfloat16)
        shape_out = (row_count, col_count, head_width)
        return (query_out.reshape(shape_out), key_out.reshape(shape_out), value_out.reshape(shape_out))
    query_all, key_all, value_all = lax.map(project, latent)
    padding = ((1, 1), (TH, TH), (0, 0), (0, 0))
    query_tiles = to_tiles(query_all, TH, TW)
    key_tiles = to_tiles(jnp.pad(key_all, padding), TH, TW)
    value_tiles = to_tiles(jnp.pad(value_all, padding), TH, TW)
    text_raw = jnp.dot(text_states, w_text, preferred_element_type=jnp.float32).astype(jnp.bfloat16)
    text_key_set = rms_norm(text_raw[:, :head_width].astype(jnp.float32), norm_gains[3]).astype(jnp.bfloat16)
    text_value_set = text_raw[:, head_width:]
    row_total = row_count // TH

    def finish(frame_index):
        key_ext = lax.dynamic_slice_in_dim(key_tiles, frame_index, 3, 0)
        value_ext = lax.dynamic_slice_in_dim(value_tiles, frame_index, 3, 0)
        attended = tile_attention(query_tiles[frame_index], key_ext, value_ext, tile_offsets[:, frame_index], 0, frame_index, frame_count, row_total)
        self_mix = from_tiles(attended, TH, TW)
        self_out = jnp.dot(self_mix, w_main[:, 4 * head_width:5 * head_width].T, preferred_element_type=jnp.float32)
        residual = latent[frame_index].reshape(-1, model_dim).astype(jnp.float32) + modulation[2] * self_out
        normed = (layer_norm(residual) * cross_norm[0] + cross_norm[1]).astype(jnp.bfloat16)
        cross_query = rms_norm(jnp.dot(normed, w_main[:, 3 * head_width:4 * head_width], preferred_element_type=jnp.float32), norm_gains[2]).astype(jnp.bfloat16)
        crossed = cross_attention(cross_query, text_key_set, text_value_set, text_mask)
        result = residual + jnp.dot(crossed, w_main[:, 5 * head_width:].T, preferred_element_type=jnp.float32)
        return result.astype(jnp.bfloat16).reshape(row_count, col_count, model_dim)
    return lax.map(finish, jnp.arange(frame_count, dtype=jnp.int32))
```

```python
import jax
import jax.numpy as jnp
from jax import lax
from jax.experimental import pallas as pl
from jax.experimental.pallas import tpu as pltpu
from jax.sharding import PartitionSpec as P

MESH = pl.DeviceIdType.MESH
BF = jnp.bfloat16
F32 = jnp.float32
TOK = 208
WIN = 640
HALF = 384
D = 1536
SCALE = 128.0**-0.5 * 1.4426950408889634
K0, V0, Q0, SO0, CQ0, TX0, CO0, END = 0, 384, 768, 1152, 1536, 1920, 2176, 2560
NSEM = 160


def layer_norm(values):
    average = jnp.mean(values, axis=-1, keepdims=True)
    centred = values - average
    variance = jnp.mean(centred * centred, axis=-1, keepdims=True)
    return centred * lax.rsqrt(variance + 1e-06)


def dot_nt(a, b):
    return lax.dot_general(a, b, (((1,), (1,)), ((), ())), preferred_element_type=F32)


def dot(a, b):
    return jnp.dot(a, b, preferred_element_type=F32)


def kernel(
    lat, mod, cn, ng, w, ts, wt, off, tmask, out,
    ga, gb, oth, modb, kvb, raw, ssb, qb, rb, mb, mixb, mixo, res, txt,
    send, recv,
):
    t = lax.axis_index("tm")
    h = lax.axis_index("height")
    c = lax.rem(h, 2)
    yhi = lax.rem(lax.div(h, 2), 2)
    z = lax.div(h, 4)
    x = lax.div(t, 2)
    ylo = lax.rem(t, 2)

    def at(dt, dh):
        return (lax.rem(t + dt + 8, 8), lax.rem(h + dh + 32, 32))

    hs = h + 1 - 2 * c
    sib = (t, hs)
    pt, ph = t + 1 - 2 * ylo, h + 2 - 4 * yhi
    pho = ph + 1 - 2 * c
    zup, zdn, xup, xdn = at(0, 4), at(0, -4), at(2, 0), at(-2, 0)
    halo = [(dt, dg) for dt in (-1, 0, 1) for dg in (-1, 0, 1) if (dt, dg) != (0, 0)]
    peers = [sib, (pt, ph), (pt, pho), zup, zdn, xup, xdn]
    peers += [at(dt, 2 * dg) for dt, dg in halo]

    def rows(start, count):
        return pl.ds(pl.multiple_of(start, 16), count)

    own = rows(48 * h, 48)
    for part, col in ((1, K0), (2, V0), (0, Q0), (4, SO0), (3, CQ0), (5, CO0)):
        mine = pl.ds(pl.multiple_of(768 * part + HALF * c, 128), HALF)
        other = pl.ds(pl.multiple_of(768 * part + HALF * (1 - c), 128), HALF)
        ga[own, pl.ds(col, HALF)] = w[:, mine]
        oth[:, pl.ds(col, HALF)] = w[:, other]

    barrier = pltpu.get_barrier_semaphore()
    for peer in peers:
        pl.semaphore_signal(barrier, inc=1, device_id=peer, device_id_type=MESH)
    pl.semaphore_wait(barrier, len(peers))

    used = [0]
    started = []

    def push(src, dst, peer, arriving):
        i = used[0]
        used[0] += 1
        copy = pltpu.make_async_remote_copy(
            src_ref=src, dst_ref=dst, send_sem=send.at[i], recv_sem=recv.at[i],
            device_id=peer, device_id_type=MESH,
        )
        copy.start()
        started.append(copy)
        arrival = pltpu.make_async_remote_copy(
            src_ref=arriving, dst_ref=arriving, send_sem=send.at[i], recv_sem=recv.at[i],
            device_id=peer, device_id_type=MESH,
        )
        return arrival.wait_recv

    slab_waits = {}

    def slab(lo, hi):
        cols = pl.ds(lo, hi - lo)
        slab_waits[lo] = [
            push(oth.at[:, cols], ga.at[own, cols], sib, ga.at[rows(48 * hs, 48), cols]),
            push(ga.at[own, cols], ga.at[own, cols], (pt, ph), ga.at[rows(48 * ph, 48), cols]),
            push(oth.at[:, cols], ga.at[own, cols], (pt, pho), ga.at[rows(48 * pho, 48), cols]),
        ]

    def slab_wait(lo):
        for wait in slab_waits[lo]:
            wait()

    def slot(step):
        return 192 * lax.rem(z + step + 8, 8)

    def ring_z(lo, hi, forward):
        cols = pl.ds(lo, hi - lo)
        slab_wait(lo)
        for s in range(4):
            a, n, b = (0, 192, 0) if s < 3 else (0, 96, 96)

            def view(step, base):
                return ga.at[rows(slot(step) + base, n), cols]

            up = push(view(-s, a), view(-s, a), zup, view(-s - 1, a))
            dn = push(view(s, b), view(s, b), zdn, view(s + 1, b))
            yield
            up()
            dn()
        yield from finish(lo, hi, forward)

    def finish(lo, hi, forward):
        if forward:
            cols, there = pl.ds(lo, hi - lo), pl.ds(lo - SO0, hi - lo)
            wait = push(ga.at[:, cols], gb.at[:, there], sib, gb.at[:, there])
            yield
            wait()

    def ring_x(lo, hi, forward):
        cols = pl.ds(lo, hi - lo)
        slab_wait(lo)

        def piece(step, quarter):
            return ga.at[rows(slot(step) + 48 * quarter, 48), cols]

        for s in range(4):
            if s < 3:
                up = push(piece(-s, x), piece(-s, x), zup, piece(-s - 1, x))
                dn = push(piece(s, x), piece(s, x), zdn, piece(s + 1, x))
                yield
                up()
                dn()
            else:
                up = push(piece(-s, x), piece(-s, x), zup, piece(-s - 1, x))
                yield
                up()
        left, right = lax.rem(x + 3, 4), lax.rem(x + 1, 4)

        def fan(quarter, slabs, peer, count):
            i = used[0]
            used[0] += 1

            def one(k, carry):
                part = piece(k, quarter)
                pltpu.make_async_remote_copy(
                    src_ref=part, dst_ref=part, send_sem=send.at[i], recv_sem=recv.at[i],
                    device_id=peer, device_id_type=MESH,
                ).start()
                return carry

            lax.fori_loop(slabs[0], slabs[1], one, 0)
            whole = ga.at[pl.ds(0, 48 * count), cols]
            copy = pltpu.make_async_remote_copy(
                src_ref=whole, dst_ref=whole, send_sem=send.at[i], recv_sem=recv.at[i],
                device_id=peer, device_id_type=MESH,
            )
            started.append(copy)
            return copy.wait_recv

        to_up = fan(x, (1, 8), xup, 7)
        to_dn = fan(x, (1, 8), xdn, 7)
        yield
        to_up()
        to_dn()
        to_up = fan(left, (1, 5), xup, 4)
        to_dn = fan(right, (5, 8), xdn, 3)
        yield
        to_up()
        to_dn()
        yield from finish(lo, hi, forward)

    chunks = ((K0, V0), (V0, Q0), (Q0, SO0), (SO0, CQ0))
    for lo, hi in chunks:
        slab(lo, hi)

    ring_k, ring_v = ring_z(K0, V0, False), ring_z(V0, Q0, False)
    ring_q, ring_so = ring_x(Q0, SO0, False), ring_z(SO0, CQ0, True)
    ring_cq, ring_co = ring_x(CQ0, CO0, True), ring_x(CO0, END, True)

    def pump(*rings):
        for ring in rings:
            next(ring, None)

    def drain(*rings):
        for ring in rings:
            for _ in ring:
                pass

    pump(ring_k, ring_v, ring_q)

    mine = rows(TOK * c, TOK)
    theirs = rows(TOK * (1 - c), TOK)
    latent = lat[...].astype(F32)
    modb[mine, :] = (layer_norm(latent) * (1.0 + mod[1:2, :]) + mod[0:1, :]).astype(BF)
    got_mod = push(modb.at[mine, :], modb.at[mine, :], sib, modb.at[theirs, :])

    txt[...] = dot_nt(wt[...], ts[...]).astype(BF)
    ga[own, pl.ds(TX0, 256)] = txt[:, pl.ds(pl.multiple_of(256 * c, 128), 256)]
    oth[:, pl.ds(TX0, 256)] = txt[:, pl.ds(pl.multiple_of(256 * (1 - c), 128), 256)]
    slab(CQ0, CO0)
    slab(CO0, END)
    pump(ring_k, ring_v, ring_q)

    lane = lax.broadcasted_iota(jnp.int32, (8, WIN), 1)
    frame = lax.broadcasted_iota(jnp.int32, (8, WIN), 0)

    def step_of(value, *edges):
        total = jnp.zeros_like(value)
        for edge in edges:
            total = total + (value >= edge).astype(jnp.int32)
        return total

    row_at = step_of(lane, 208, 416)
    within = lane - 208 * row_at
    within = within - 104 * step_of(within, 104)
    code = jnp.where(lane < 624, 12 * frame + 4 * row_at + step_of(within, 26, 52, 78), -2)
    for q in range(4):
        allowed = code == 16 + q
        for j in range(8):
            dt, dr, dc = off[0, 0, 0, q, j], off[1, 0, 0, q, j], off[2, 0, 0, q, j]
            ft, rt, ct = t + dt, h + dr, q + dc
            usable = (ft >= 0) & (ft < 8) & (rt >= 0) & (rt < 32) & (ct >= 0) & (ct < 4)
            target = jnp.where(usable, 12 * (dt + 1) + 4 * (dr + 1) + ct, -1)
            allowed = allowed | (code == target)
        rb[c, pl.ds(8 * q, 8), :] = jnp.where(allowed, 0.0, -jnp.inf).astype(F32)
    got_rb = push(rb.at[c], rb.at[c], sib, rb.at[1 - c])
    pump(ring_k, ring_v, ring_q)
    got_rb()
    token = lax.broadcasted_iota(jnp.int32, (TOK, 1), 0)
    token = token - 104 * step_of(token, 104)
    tile = step_of(token, 26, 52, 78)

    def masks(i, carry):
        r, f = lax.div(i, 3), lax.rem(i, 3)
        picked = rb[r, pl.ds(f, 1), :]
        for q in range(1, 4):
            picked = jnp.where(tile == q, rb[r, pl.ds(8 * q + f, 1), :], picked)
        mb[r, f] = jnp.broadcast_to(picked, (TOK, WIN))
        return carry

    lax.fori_loop(0, 6, masks, 0)
    for f in range(3):
        kvb[f, pl.ds(832, 16), :] = jnp.zeros((16, 768), BF)
    pump(ring_k, ring_v, ring_q)
    got_mod()
    drain(ring_k, ring_v)
    pump(ring_so, ring_cq, ring_co)

    both = pl.ds(TOK, 2 * TOK)
    raw[...] = dot(modb[...], ga[:, pl.ds(K0, HALF)])

    def squares(i):
        ssb[i, 0] = jnp.broadcast_to(
            jnp.sum(raw[...] * raw[...], axis=-1, keepdims=True), (2 * TOK, 128)
        )
        return push(ssb.at[i, 0], ssb.at[i, 1], sib, ssb.at[i, 1])

    def gain(i, half):
        return ng[i : i + 1, pl.ds(pl.multiple_of(HALF * half, 128), HALF)]

    def normal(i, gains):
        total = ssb[i, 0, :, 0:1] + ssb[i, 1, :, 0:1]
        return raw[...] * lax.rsqrt(total * (1.0 / 768) + 1e-06) * gains

    def send_halo(lo):
        cols = pl.ds(lo, HALF)
        waits = []
        for dt, dg in halo:
            first, count = (TOK, 2 * TOK) if dg == 0 else (2 * TOK, TOK) if dg > 0 else (TOK, TOK)
            there = TOK if dg == 0 else 0 if dg > 0 else 3 * TOK
            src = kvb.at[1, pl.ds(first, count), cols]
            dst = kvb.at[1 - dt, pl.ds(there, count), cols]
            waits.append(push(src, dst, at(dt, 2 * dg), dst))
        return waits

    got_k_squares = squares(0)
    kvb[1, both, pl.ds(HALF, HALF)] = dot(modb[...], ga[:, pl.ds(V0, HALF)]).astype(BF)
    v_waits = send_halo(HALF)
    got_k_squares()
    kvb[1, both, pl.ds(0, HALF)] = normal(0, gain(1, c)).astype(BF)
    k_waits = send_halo(0)

    drain(ring_q)
    pump(ring_so, ring_cq, ring_co)
    raw[...] = dot(modb[...], ga[:, pl.ds(Q0, HALF)])
    got_q_squares = squares(1)
    pump(ring_so, ring_cq, ring_co)
    got_q_squares()
    qb[...] = normal(1, gain(0, c) * SCALE).astype(BF)
    for _ in range(4):
        pump(ring_so, ring_cq, ring_co)
    for wait in v_waits + k_waits:
        wait()

    def attend(r, i):
        q = qb[pl.ds(TOK * r, TOK), pl.ds(128 * i, 128)]
        keys = pl.ds(TOK * r, WIN)
        scores = [dot_nt(q, kvb[f, keys, pl.ds(128 * i, 128)]) + mb[r, f] for f in range(3)]
        largest = jnp.max(scores[0], axis=-1, keepdims=True)
        for s in scores[1:]:
            largest = jnp.maximum(largest, jnp.max(s, axis=-1, keepdims=True))
        total, mixed = 0.0, 0.0
        for f in range(3):
            p = jnp.exp2(scores[f] - largest)
            total = total + jnp.sum(p, axis=-1, keepdims=True)
            mixed = mixed + dot(p.astype(BF), kvb[f, keys, pl.ds(HALF + 128 * i, 128)])
        mixb[pl.ds(TOK * r, TOK), pl.ds(128 * i, 128)] = (mixed / total).astype(BF)

    for r in range(2):
        for i in range(3):
            attend(r, i)
            pump(ring_so, ring_cq, ring_co)
    got_mix = push(mixb.at[theirs, :], mixo, sib, mixo)
    drain(ring_so)
    got_mix()

    def outward(mine_in, other_in, lo, i):
        n = pl.ds(pl.multiple_of(256 * i, 256), 256)
        return dot_nt(mine_in, ga[n, pl.ds(lo, HALF)]) + dot_nt(
            other_in, gb[n, pl.ds(lo - SO0, HALF)]
        )

    mix_mine, mix_other = mixb[mine, :], mixo[...]

    def self_out(i, carry):
        n = pl.ds(pl.multiple_of(256 * i, 256), 256)
        res[:, n] = lat[:, n].astype(F32) + mod[2:3, n] * outward(mix_mine, mix_other, SO0, i)
        return carry

    lax.fori_loop(0, 6, self_out, 0)
    drain(ring_cq)
    normed = (layer_norm(res[...]) * cn[0:1, :] + cn[1:2, :]).astype(BF)
    cq_mine = dot(normed, ga[:, pl.ds(CQ0, HALF)])
    cq_other = dot(normed, gb[:, pl.ds(CQ0 - SO0, HALF)])
    square = jnp.sum(cq_mine * cq_mine, axis=-1, keepdims=True)
    square = square + jnp.sum(cq_other * cq_other, axis=-1, keepdims=True)
    inverse = lax.rsqrt(square * (1.0 / 768) + 1e-06) * SCALE
    raw[0:TOK, :] = cq_mine * inverse * (gain(2, c) * gain(3, c))
    raw[TOK : 2 * TOK, :] = cq_other * inverse * (gain(2, 1 - c) * gain(3, 1 - c))

    def text_scale(ref, lo):
        keys = ref[0:768, pl.ds(lo, 256)].astype(F32)
        return lax.rsqrt(jnp.sum(keys * keys, axis=0, keepdims=True) * (1.0 / 768) + 1e-06)

    real = [tmask[pl.ds(c, 1), :] == 1, tmask[pl.ds(1 - c, 1), :] == 1]
    parts = [(ga, TX0), (gb, TX0 - SO0)]
    scales = [text_scale(*part) for part in parts]
    for k in range(2):
        base = HALF * c if k == 0 else HALF * (1 - c)
        for i in range(3):
            q = raw[pl.ds(TOK * k, TOK), pl.ds(128 * i, 128)].astype(BF)
            krow, vrow = rows(base + 128 * i, 128), rows(768 + base + 128 * i, 128)
            scores = [
                jnp.where(real[j], dot(q, ref[krow, pl.ds(lo, 256)]) * scales[j], -jnp.inf)
                for j, (ref, lo) in enumerate(parts)
            ]
            largest = jnp.maximum(
                jnp.max(scores[0], axis=-1, keepdims=True),
                jnp.max(scores[1], axis=-1, keepdims=True),
            )
            total, mixed = 0.0, 0.0
            for j, (ref, lo) in enumerate(parts):
                p = jnp.exp2(scores[j] - largest)
                total = total + jnp.sum(p, axis=-1, keepdims=True)
                mixed = mixed + dot_nt(p.astype(BF), ref[vrow, pl.ds(lo, 256)])
            qb[pl.ds(TOK * k, TOK), pl.ds(128 * i, 128)] = (mixed / total).astype(BF)
    drain(ring_co)
    cross_mine, cross_other = qb[0:TOK, :], qb[TOK : 2 * TOK, :]

    def cross_out(i, carry):
        n = pl.ds(pl.multiple_of(256 * i, 256), 256)
        out[:, n] = (res[:, n] + outward(cross_mine, cross_other, CO0, i)).astype(BF)
        return carry

    lax.fori_loop(0, 6, cross_out, 0)
    for copy in started:
        copy.wait_send()


def body(
    latent, modulation, cross_norm, norm_gains, w_main, text_states, w_text, tile_offsets, text_mask
):
    vmem = pl.BlockSpec(memory_space=pltpu.VMEM)
    smem = pl.BlockSpec(memory_space=pltpu.SMEM)
    result = pl.pallas_call(
        kernel,
        out_shape=jax.ShapeDtypeStruct((TOK, D), BF),
        in_specs=[vmem] * 7 + [smem, vmem],
        out_specs=vmem,
        scratch_shapes=[
            pltpu.VMEM((D, END), BF),
            pltpu.VMEM((D, END - SO0), BF),
            pltpu.VMEM((48, END), BF),
            pltpu.VMEM((2 * TOK, D), BF),
            pltpu.VMEM((3, 848, 768), BF),
            pltpu.VMEM((2 * TOK, HALF), F32),
            pltpu.VMEM((2, 2, 2 * TOK, 128), F32),
            pltpu.VMEM((2 * TOK, HALF), BF),
            pltpu.VMEM((2, 32, WIN), F32),
            pltpu.VMEM((2, 3, TOK, WIN), F32),
            pltpu.VMEM((2 * TOK, HALF), BF),
            pltpu.VMEM((TOK, HALF), BF),
            pltpu.VMEM((TOK, D), F32),
            pltpu.VMEM((48, 512), BF),
            pltpu.SemaphoreType.DMA((NSEM,)),
            pltpu.SemaphoreType.DMA((NSEM,)),
        ],
        compiler_params=pltpu.CompilerParams(
            collective_id=0, has_side_effects=True, vmem_limit_bytes=60 * 1024 * 1024
        ),
        cost_estimate=pl.CostEstimate(
            flops=6_000_000_000, bytes_accessed=6_000_000, transcendentals=3_000_000
        ),
    )(
        latent.reshape(TOK, D),
        modulation,
        cross_norm,
        norm_gains,
        w_main,
        text_states,
        w_text.T,
        tile_offsets,
        text_mask.reshape(2, 256),
    )
    return result.reshape(latent.shape)


def solution(mesh):
    placed = (
        P("tm", "height", None, None),
        P(),
        P(),
        P(),
        P("height", None),
        P(),
        P(None, "height"),
        P(None, "tm", "height", None, None),
        P(),
    )
    return jax.shard_map(
        body, mesh=mesh, in_specs=placed, out_specs=P("tm", "height", None, None), check_vma=False
    )
```

```python
import jax
import jax.numpy as jnp
from jax import lax
from jax.experimental import pallas as pl
from jax.experimental.pallas import tpu as pltpu
from jax.sharding import PartitionSpec as P

MESH = pl.DeviceIdType.MESH
BF = jnp.bfloat16
F32 = jnp.float32
TOK = 208
WIN = 640
HALF = 384
D = 1536
SCALE = 128.0**-0.5 * 1.4426950408889634
K0, V0, Q0, SO0, CQ0, TX0, CO0, END = 0, 384, 768, 1152, 1536, 1920, 2176, 2560
NSEM = 160


def layer_norm(values):
    average = jnp.mean(values, axis=-1, keepdims=True)
    centred = values - average
    variance = jnp.mean(centred * centred, axis=-1, keepdims=True)
    return centred * lax.rsqrt(variance + 1e-06)


def dot_nt(a, b):
    return lax.dot_general(a, b, (((1,), (1,)), ((), ())), preferred_element_type=F32)


def dot(a, b):
    return jnp.dot(a, b, preferred_element_type=F32)


def kernel(
    lat_in, mod, cn, ng, w_in, ts_in, wt_in, off, tmask, out,
    lat, w, ts, wt, ga, gb, oth, modb, lats, kvb, kraw, ssb, raw, ssq, qb, rb, mb, mixb, mixo, res, txt,
    send, recv, load,
):
    t = lax.axis_index("tm")
    h = lax.axis_index("height")
    c = lax.rem(h, 2)
    yhi = lax.rem(lax.div(h, 2), 2)
    z = lax.div(h, 4)
    x = lax.div(t, 2)
    ylo = lax.rem(t, 2)

    loads = [
        pltpu.make_async_copy(src, dst, load.at[i])
        for i, (src, dst) in enumerate(((w_in, w), (lat_in, lat), (wt_in, wt), (ts_in, ts)))
    ]
    for copy in loads:
        copy.start()

    def at(dt, dh):
        return (lax.rem(t + dt + 8, 8), lax.rem(h + dh + 32, 32))

    hs = h + 1 - 2 * c
    sib = (t, hs)
    pt, ph = t + 1 - 2 * ylo, h + 2 - 4 * yhi
    pho = ph + 1 - 2 * c
    zup, zdn, xup, xdn = at(0, 4), at(0, -4), at(2, 0), at(-2, 0)
    edge = 2 * c - 1
    peers = [sib, (pt, ph), (pt, pho), zup, zdn, xup, xdn, at(-1, 0), at(1, 0)]
    peers += [at(dt, edge) for dt in (-1, 0, 1)]

    barrier = pltpu.get_barrier_semaphore()
    for peer in peers:
        pl.semaphore_signal(barrier, inc=1, device_id=peer, device_id_type=MESH)

    def rows(start, count):
        return pl.ds(pl.multiple_of(start, 16), count)

    own = rows(48 * h, 48)

    def keep(col, values):
        ga[own, pl.ds(col, values.shape[1])] = values

    loads[0].wait()
    for part, col in ((1, K0), (2, V0), (0, Q0), (4, SO0), (3, CQ0), (5, CO0)):
        mine = pl.ds(pl.multiple_of(768 * part + HALF * c, 128), HALF)
        other = pl.ds(pl.multiple_of(768 * part + HALF * (1 - c), 128), HALF)
        oth[:, pl.ds(col, HALF)] = w[:, other]
        if col in (K0, V0, SO0):
            ga[own, pl.ds(col, HALF)] = w[:, mine]
        else:
            pl.when(lax.rem(h, 4) == x)(lambda col=col, mine=mine: keep(col, w[:, mine]))
    pl.semaphore_wait(barrier, len(peers))

    used = [0]
    started = []

    def index():
        used[0] += 1
        return used[0] - 1

    def remote(src, dst, peer, i):
        return pltpu.make_async_remote_copy(
            src_ref=src, dst_ref=dst, send_sem=send.at[i], recv_sem=recv.at[i],
            device_id=peer, device_id_type=MESH,
        )

    def push(src, dst, peer, arriving):
        i = index()
        copy = remote(src, dst, peer, i)
        copy.start()
        started.append(copy.wait_send)
        return remote(arriving, arriving, peer, i).wait_recv

    slab_waits = {}

    def slab(lo, hi):
        cols = pl.ds(lo, hi - lo)
        slab_waits[lo] = [
            push(oth.at[:, cols], ga.at[own, cols], sib, ga.at[rows(48 * hs, 48), cols]),
            push(ga.at[own, cols], ga.at[own, cols], (pt, ph), ga.at[rows(48 * ph, 48), cols]),
            push(oth.at[:, cols], ga.at[own, cols], (pt, pho), ga.at[rows(48 * pho, 48), cols]),
        ]

    def slab_one(lo, hi):
        cols = pl.ds(lo, hi - lo)
        piece = lax.rem(h, 4)
        whole = ga.at[own, cols]
        waits = []
        for src, peer, row in (
            (oth.at[:, cols], sib, hs),
            (whole, (pt, ph), ph),
            (oth.at[:, cols], (pt, pho), pho),
        ):
            copy = remote(src, whole, peer, index())
            pl.when(piece == x)(copy.start)
            started.append(lambda copy=copy: pl.when(piece == x)(copy.wait_send))
            landed = ga.at[rows(48 * row, 48), cols]
            arrival = remote(landed, landed, peer, used[0] - 1)
            waits.append(
                lambda arrival=arrival, row=row: pl.when(lax.rem(row, 4) == x)(arrival.wait_recv)
            )
        slab_waits[lo] = waits

    def slab_wait(lo):
        for wait in slab_waits[lo]:
            wait()

    def slot(step):
        return 192 * lax.rem(z + step + 8, 8)

    def ring_z(lo, hi, forward):
        cols = pl.ds(lo, hi - lo)
        slab_wait(lo)
        for s in range(4):
            a, n, b = (0, 192, 0) if s < 3 else (0, 96, 96)

            def view(step, base):
                return ga.at[rows(slot(step) + base, n), cols]

            up = push(view(-s, a), view(-s, a), zup, view(-s - 1, a))
            dn = push(view(s, b), view(s, b), zdn, view(s + 1, b))
            yield
            up()
            dn()
        yield from finish(lo, hi, forward)

    def finish(lo, hi, forward):
        if forward:
            cols, there = pl.ds(lo, hi - lo), pl.ds(lo - SO0, hi - lo)
            wait = push(ga.at[:, cols], gb.at[:, there], sib, gb.at[:, there])
            yield
            wait()

    def ring_x(lo, hi, forward):
        cols = pl.ds(lo, hi - lo)
        slab_wait(lo)

        def piece(step, quarter):
            return ga.at[rows(slot(step) + 48 * quarter, 48), cols]

        for s in range(4):
            up = push(piece(-s, x), piece(-s, x), zup, piece(-s - 1, x))
            dn = None
            if s < 3:
                dn = push(piece(s, x), piece(s, x), zdn, piece(s + 1, x))
            yield
            up()
            if s < 3:
                dn()
        left, right = lax.rem(x + 3, 4), lax.rem(x + 1, 4)

        def fan(quarter, slabs, peer):
            i = index()

            def one(k, carry):
                part = piece(k, quarter)
                remote(part, part, peer, i).start()
                return carry

            lax.fori_loop(slabs[0], slabs[1], one, 0)
            whole = ga.at[pl.ds(0, 48 * (slabs[1] - slabs[0])), cols]
            copy = remote(whole, whole, peer, i)
            started.append(copy.wait_send)
            return copy.wait_recv

        to_up = fan(x, (0, 8), xup)
        to_dn = fan(x, (0, 8), xdn)
        yield
        to_up()
        to_dn()
        to_up = fan(left, (0, 4), xup)
        to_dn = fan(right, (4, 8), xdn)
        yield
        to_up()
        to_dn()
        yield from finish(lo, hi, forward)

    def send_latent():
        waits = []
        for place, dt, dh in ((1, -1, 0), (0, 1, 0), (4, -1, edge), (3, 0, edge), (2, 1, edge)):
            waits.append((place, push(lat_in, lats.at[place], at(dt, dh), lats.at[place])))
        return dict(waits)

    slab(K0, V0)
    slab(V0, Q0)
    slab_one(Q0, SO0)
    slab(SO0, CQ0)
    got_latent = send_latent()

    rings = {
        "k": ring_z(K0, V0, False),
        "v": ring_z(V0, Q0, False),
        "q": ring_x(Q0, SO0, False),
        "so": ring_z(SO0, CQ0, True),
        "cq": ring_x(CQ0, CO0, True),
        "co": ring_x(CO0, END, True),
    }

    def pump(*names):
        for name in names:
            next(rings[name], None)

    def drain(*names):
        for name in names:
            for _ in rings[name]:
                pass

    pump("k", "v", "q")

    shown = [(0, 1 + c), (2, 1 + c), (0, 3 * c), (1, 3 * c), (2, 3 * c), (1, 1 + c)]
    hidden = [(0, 2 - c), (2, 2 - c), (0, 3 - 3 * c), (1, 3 - 3 * c), (2, 3 - 3 * c), (1, 2 - c)]
    got_mod = {}

    def modulate(place, src):
        f, r = shown[place]
        here = modb.at[f, rows(TOK * r, TOK)]
        values = layer_norm(src[...].astype(F32)) * (1.0 + mod[1:2, :]) + mod[0:1, :]
        here[...] = values.astype(BF)
        f, r = hidden[place]
        got_mod[place] = push(here, here, sib, modb.at[f, rows(TOK * r, TOK)])

    def modulate_halo(place):
        got_latent[place]()
        modulate(place, lats.at[place])

    loads[1].wait()
    modulate(5, lat)

    loads[2].wait()
    loads[3].wait()
    txt[...] = dot_nt(wt[...], ts[...]).astype(BF)
    mine = pl.ds(pl.multiple_of(256 * c, 128), 256)
    pl.when(lax.rem(h, 4) == x)(lambda mine=mine: keep(TX0, txt[:, mine]))
    oth[:, pl.ds(TX0, 256)] = txt[:, pl.ds(pl.multiple_of(256 * (1 - c), 128), 256)]
    slab_one(CQ0, CO0)
    slab_one(CO0, END)
    pump("k", "v", "q")

    lane = lax.broadcasted_iota(jnp.int32, (8, WIN), 1)
    frame = lax.broadcasted_iota(jnp.int32, (8, WIN), 0)

    def step_of(value, *edges):
        total = jnp.zeros_like(value)
        for mark_at in edges:
            total = total + (value >= mark_at).astype(jnp.int32)
        return total

    row_at = step_of(lane, 208, 416)
    within = lane - 208 * row_at
    within = within - 104 * step_of(within, 104)
    code = jnp.where(lane < 624, 12 * frame + 4 * row_at + step_of(within, 26, 52, 78), -2)
    for q in range(4):
        allowed = code == 16 + q
        for j in range(8):
            dt, dr, dc = off[0, 0, 0, q, j], off[1, 0, 0, q, j], off[2, 0, 0, q, j]
            ft, rt, ct = t + dt, h + dr, q + dc
            usable = (ft >= 0) & (ft < 8) & (rt >= 0) & (rt < 32) & (ct >= 0) & (ct < 4)
            target = jnp.where(usable, 12 * (dt + 1) + 4 * (dr + 1) + ct, -1)
            allowed = allowed | (code == target)
        rb[c, pl.ds(8 * q, 8), :] = jnp.where(allowed, 0.0, -jnp.inf).astype(F32)
    got_rb = push(rb.at[c], rb.at[c], sib, rb.at[1 - c])
    got_rb()
    token = lax.broadcasted_iota(jnp.int32, (TOK, 1), 0)
    token = token - 104 * step_of(token, 104)
    tile = step_of(token, 26, 52, 78)

    def masks(i, carry):
        r, f = lax.div(i, 3), lax.rem(i, 3)
        picked = rb[r, pl.ds(f, 1), :]
        for q in range(1, 4):
            picked = jnp.where(tile == q, rb[r, pl.ds(8 * q + f, 1), :], picked)
        mb[r, f] = jnp.broadcast_to(picked, (TOK, WIN))
        return carry

    lax.fori_loop(0, 6, masks, 0)
    for f in range(3):
        kvb[f, pl.ds(832, 16), :] = jnp.zeros((16, 768), BF)
    pump("k", "v", "q")

    def gain(i, half):
        return ng[i : i + 1, pl.ds(pl.multiple_of(HALF * half, 128), HALF)]

    def squares(values, mine_at, theirs_at):
        total = jnp.sum(values * values, axis=-1, keepdims=True)
        mine_at[...] = jnp.broadcast_to(total, mine_at.shape)
        return push(mine_at, theirs_at, sib, theirs_at)

    def inverse_rms(mine_at, theirs_at):
        total = mine_at[:, 0:1] + theirs_at[:, 0:1]
        return lax.rsqrt(total * (1.0 / 768) + 1e-06)

    got_squares = {}

    def keys_values(f, r, n):
        here, flat = pl.ds(TOK * r, TOK * n), pl.ds(TOK * (4 * f + r), TOK * n)
        modulated = modb[f, here, :]
        keys = dot(modulated, ga[:, pl.ds(K0, HALF)])
        kraw[flat, :] = keys
        got_squares[f, r, n] = squares(keys, ssb.at[0, flat], ssb.at[1, flat])
        kvb[f, here, pl.ds(HALF, HALF)] = dot(modulated, ga[:, pl.ds(V0, HALF)]).astype(BF)

    def normal_keys(f, r, n):
        here, flat = pl.ds(TOK * r, TOK * n), pl.ds(TOK * (4 * f + r), TOK * n)
        got_squares[f, r, n]()
        scaled = kraw[flat, :] * inverse_rms(ssb.at[0, flat], ssb.at[1, flat])
        kvb[f, here, pl.ds(0, HALF)] = (scaled * gain(1, c)).astype(BF)

    both = pl.ds(TOK, 2 * TOK)
    got_queries = []

    def queries():
        raw[...] = dot(modb[1, both, :], ga[:, pl.ds(Q0, HALF)])
        got_queries.append(squares(raw[...], ssq.at[0], ssq.at[1]))

    def normal_queries():
        got_queries[0]()
        qb[...] = (raw[...] * inverse_rms(ssq.at[0], ssq.at[1]) * (gain(0, c) * SCALE)).astype(BF)

    pump("k", "v", "q")
    modulate_halo(0)
    modulate_halo(1)
    drain("k", "v")
    pump("so", "cq", "co", "q")
    got_mod[5]()
    keys_values(1, 1, 2)
    pump("cq", "co", "so")
    got_mod[0]()
    keys_values(0, 1, 2)
    normal_keys(1, 1, 2)
    got_mod[1]()
    keys_values(2, 1, 2)
    normal_keys(0, 1, 2)
    pump("cq", "co", "so", "q")
    normal_keys(2, 1, 2)
    pump("cq", "co", "so")
    drain("q")
    queries()
    pump("cq", "co", "so")
    for place in (2, 3, 4):
        modulate_halo(place)
    normal_queries()
    for f in range(3):
        got_mod[2 + f]()
        keys_values(f, 0, 1)
        keys_values(f, 3, 1)
        if f == 0:
            pump("cq", "co", "so")
    for f in range(3):
        normal_keys(f, 0, 1)
        normal_keys(f, 3, 1)

    def attend(r, i):
        q = qb[pl.ds(TOK * r, TOK), pl.ds(128 * i, 128)]
        keys = pl.ds(TOK * r, WIN)
        scores = [dot_nt(q, kvb[f, keys, pl.ds(128 * i, 128)]) + mb[r, f] for f in range(3)]
        largest = jnp.max(scores[0], axis=-1, keepdims=True)
        for s in scores[1:]:
            largest = jnp.maximum(largest, jnp.max(s, axis=-1, keepdims=True))
        total, mixed = 0.0, 0.0
        for f in range(3):
            p = jnp.exp2(scores[f] - largest)
            total = total + jnp.sum(p, axis=-1, keepdims=True)
            mixed = mixed + dot(p.astype(BF), kvb[f, keys, pl.ds(HALF + 128 * i, 128)])
        mixb[pl.ds(TOK * r, TOK), pl.ds(128 * i, 128)] = (mixed / total).astype(BF)

    for r in range(2):
        for i in range(3):
            attend(r, i)
            pump("cq", "co", "so")
    mine = rows(TOK * c, TOK)
    theirs = rows(TOK * (1 - c), TOK)
    got_mix = push(mixb.at[theirs, :], mixo, sib, mixo)
    drain("so")
    got_mix()

    def outward(mine_in, other_in, lo, i):
        n = pl.ds(pl.multiple_of(256 * i, 256), 256)
        return dot_nt(mine_in, ga[n, pl.ds(lo, HALF)]) + dot_nt(
            other_in, gb[n, pl.ds(lo - SO0, HALF)]
        )

    mix_mine, mix_other = mixb[mine, :], mixo[...]

    def self_out(i, carry):
        n = pl.ds(pl.multiple_of(256 * i, 256), 256)
        res[:, n] = lat[:, n].astype(F32) + mod[2:3, n] * outward(mix_mine, mix_other, SO0, i)
        return carry

    lax.fori_loop(0, 6, self_out, 0)
    drain("cq")
    normed = (layer_norm(res[...]) * cn[0:1, :] + cn[1:2, :]).astype(BF)
    cq_mine = dot(normed, ga[:, pl.ds(CQ0, HALF)])
    cq_other = dot(normed, gb[:, pl.ds(CQ0 - SO0, HALF)])
    square = jnp.sum(cq_mine * cq_mine, axis=-1, keepdims=True)
    square = square + jnp.sum(cq_other * cq_other, axis=-1, keepdims=True)
    inverse = lax.rsqrt(square * (1.0 / 768) + 1e-06) * SCALE
    raw[0:TOK, :] = cq_mine * inverse * (gain(2, c) * gain(3, c))
    raw[TOK : 2 * TOK, :] = cq_other * inverse * (gain(2, 1 - c) * gain(3, 1 - c))

    def text_scale(ref, lo):
        keys = ref[0:768, pl.ds(lo, 256)].astype(F32)
        return lax.rsqrt(jnp.sum(keys * keys, axis=0, keepdims=True) * (1.0 / 768) + 1e-06)

    real = [
        tmask[:, pl.ds(pl.multiple_of(256 * half, 128), 256)] == 1 for half in (c, 1 - c)
    ]
    parts = [(ga, TX0), (gb, TX0 - SO0)]
    scales = [text_scale(*part) for part in parts]
    for k in range(2):
        base = HALF * c if k == 0 else HALF * (1 - c)
        for i in range(3):
            q = raw[pl.ds(TOK * k, TOK), pl.ds(128 * i, 128)].astype(BF)
            krow, vrow = rows(base + 128 * i, 128), rows(768 + base + 128 * i, 128)
            scores = [
                jnp.where(real[j], dot(q, ref[krow, pl.ds(lo, 256)]) * scales[j], -jnp.inf)
                for j, (ref, lo) in enumerate(parts)
            ]
            largest = jnp.maximum(
                jnp.max(scores[0], axis=-1, keepdims=True),
                jnp.max(scores[1], axis=-1, keepdims=True),
            )
            total, mixed = 0.0, 0.0
            for j, (ref, lo) in enumerate(parts):
                p = jnp.exp2(scores[j] - largest)
                total = total + jnp.sum(p, axis=-1, keepdims=True)
                mixed = mixed + dot_nt(p.astype(BF), ref[vrow, pl.ds(lo, 256)])
            qb[pl.ds(TOK * k, TOK), pl.ds(128 * i, 128)] = (mixed / total).astype(BF)
    drain("co")
    cross_mine, cross_other = qb[0:TOK, :], qb[TOK : 2 * TOK, :]

    def cross_out(i, carry):
        n = pl.ds(pl.multiple_of(256 * i, 256), 256)
        out[:, n] = (res[:, n] + outward(cross_mine, cross_other, CO0, i)).astype(BF)
        return carry

    lax.fori_loop(0, 6, cross_out, 0)
    assert used[0] <= NSEM
    for wait in started:
        wait()


def body(
    latent, modulation, cross_norm, norm_gains, w_main, text_states, w_text, tile_offsets, text_mask
):
    vmem = pl.BlockSpec(memory_space=pltpu.VMEM)
    smem = pl.BlockSpec(memory_space=pltpu.SMEM)
    hbm = pl.BlockSpec(memory_space=pl.ANY)
    result = pl.pallas_call(
        kernel,
        out_shape=jax.ShapeDtypeStruct((TOK, D), BF),
        in_specs=[hbm, vmem, vmem, vmem, hbm, hbm, hbm, smem, vmem],
        out_specs=vmem,
        scratch_shapes=[
            pltpu.VMEM((TOK, D), BF),
            pltpu.VMEM((48, 4608), BF),
            pltpu.VMEM((512, D), BF),
            pltpu.VMEM((48, D), BF),
            pltpu.VMEM((D, END), BF),
            pltpu.VMEM((D, END - SO0), BF),
            pltpu.VMEM((48, END), BF),
            pltpu.VMEM((3, 4 * TOK, D), BF),
            pltpu.VMEM((5, TOK, D), BF),
            pltpu.VMEM((3, 848, 768), BF),
            pltpu.VMEM((12 * TOK, HALF), F32),
            pltpu.VMEM((2, 12 * TOK, 128), F32),
            pltpu.VMEM((2 * TOK, HALF), F32),
            pltpu.VMEM((2, 2 * TOK, 128), F32),
            pltpu.VMEM((2 * TOK, HALF), BF),
            pltpu.VMEM((2, 32, WIN), F32),
            pltpu.VMEM((2, 3, TOK, WIN), F32),
            pltpu.VMEM((2 * TOK, HALF), BF),
            pltpu.VMEM((TOK, HALF), BF),
            pltpu.VMEM((TOK, D), F32),
            pltpu.VMEM((48, 512), BF),
            pltpu.SemaphoreType.DMA((NSEM,)),
            pltpu.SemaphoreType.DMA((NSEM,)),
            pltpu.SemaphoreType.DMA((4,)),
        ],
        compiler_params=pltpu.CompilerParams(
            collective_id=0, has_side_effects=True, vmem_limit_bytes=60 * 1024 * 1024
        ),
        cost_estimate=pl.CostEstimate(
            flops=6_000_000_000, bytes_accessed=6_000_000, transcendentals=3_000_000
        ),
    )(
        latent.reshape(TOK, D),
        modulation,
        cross_norm,
        norm_gains,
        w_main,
        text_states,
        w_text.T,
        tile_offsets,
        text_mask.reshape(1, 512),
    )
    return result.reshape(latent.shape)


def solution(mesh):
    placed = (
        P("tm", "height", None, None),
        P(),
        P(),
        P(),
        P("height", None),
        P(),
        P(None, "height"),
        P(None, "tm", "height", None, None),
        P(),
    )
    return jax.shard_map(
        body, mesh=mesh, in_specs=placed, out_specs=P("tm", "height", None, None), check_vma=False
    )
```

```python
import jax
import jax.numpy as jnp
from jax import lax
from jax.experimental import pallas as pl
from jax.experimental.pallas import tpu as pltpu
from jax.sharding import PartitionSpec as P

MESH = pl.DeviceIdType.MESH
BF = jnp.bfloat16
F32 = jnp.float32
TOK = 208
WIN = 640
HALF = 384
D = 1536
SCALE = 128.0**-0.5 * 1.4426950408889634
K0, V0, Q0, SO0, CQ0, TX0, CO0, END = 0, 384, 768, 1152, 1536, 1920, 2176, 2560
NSEM = 160


def layer_norm(values):
    average = jnp.mean(values, axis=-1, keepdims=True)
    centred = values - average
    variance = jnp.mean(centred * centred, axis=-1, keepdims=True)
    return centred * lax.rsqrt(variance + 1e-06)


def dot_nt(a, b):
    return lax.dot_general(a, b, (((1,), (1,)), ((), ())), preferred_element_type=F32)


def dot(a, b):
    return jnp.dot(a, b, preferred_element_type=F32)


def kernel(
    lat_in, mod, cn, ng, w_in, ts_in, wt_in, off, tmask, out,
    lat, w, ts, wt, ga, gb, oth, modb, lats, kvb, kraw, ssb, raw, ssq, qb, rb, mb, mixb, mixo, res, txt,
    send, recv, load,
):
    t = lax.axis_index("tm")
    h = lax.axis_index("height")
    c = lax.rem(h, 2)
    yhi = lax.rem(lax.div(h, 2), 2)
    z = lax.div(h, 4)
    x = lax.div(t, 2)
    ylo = lax.rem(t, 2)

    loads = [
        pltpu.make_async_copy(src, dst, load.at[i])
        for i, (src, dst) in enumerate(((w_in, w), (lat_in, lat), (wt_in, wt), (ts_in, ts)))
    ]
    for copy in loads:
        copy.start()

    def at(dt, dh):
        return (lax.rem(t + dt + 8, 8), lax.rem(h + dh + 32, 32))

    hs = h + 1 - 2 * c
    sib = (t, hs)
    pt, ph = t + 1 - 2 * ylo, h + 2 - 4 * yhi
    pho = ph + 1 - 2 * c
    zup, zdn, xup, xdn = at(0, 4), at(0, -4), at(2, 0), at(-2, 0)
    edge = 2 * c - 1
    flip, outer, beyond = at(1 - 2 * ylo, 0), at(2 * ylo - 1, 0), at(2 - 4 * ylo, 0)
    peers = [sib, (pt, ph), (pt, pho), zup, zdn, xup, xdn, flip, outer, at(0, edge)]

    barrier = pltpu.get_barrier_semaphore()
    for peer in peers:
        pl.semaphore_signal(barrier, inc=1, device_id=peer, device_id_type=MESH)

    def rows(start, count):
        return pl.ds(pl.multiple_of(start, 16), count)

    own = rows(48 * h, 48)

    def keep(col, values):
        ga[own, pl.ds(col, values.shape[1])] = values

    loads[0].wait()
    for part, col in ((1, K0), (2, V0), (0, Q0), (4, SO0), (3, CQ0), (5, CO0)):
        mine = pl.ds(pl.multiple_of(768 * part + HALF * c, 128), HALF)
        other = pl.ds(pl.multiple_of(768 * part + HALF * (1 - c), 128), HALF)
        oth[:, pl.ds(col, HALF)] = w[:, other]
        if col in (K0, V0, SO0):
            ga[own, pl.ds(col, HALF)] = w[:, mine]
        else:
            pl.when(lax.rem(h, 4) == x)(lambda col=col, mine=mine: keep(col, w[:, mine]))
    pl.semaphore_wait(barrier, len(peers))

    used = [0]
    started = []

    def index():
        used[0] += 1
        return used[0] - 1

    def remote(src, dst, peer, i):
        return pltpu.make_async_remote_copy(
            src_ref=src, dst_ref=dst, send_sem=send.at[i], recv_sem=recv.at[i],
            device_id=peer, device_id_type=MESH,
        )

    def push(src, dst, peer, arriving):
        i = index()
        copy = remote(src, dst, peer, i)
        copy.start()
        started.append(copy.wait_send)
        return remote(arriving, arriving, peer, i).wait_recv

    slab_waits = {}

    def slab(lo, hi):
        cols = pl.ds(lo, hi - lo)
        slab_waits[lo] = [
            push(oth.at[:, cols], ga.at[own, cols], sib, ga.at[rows(48 * hs, 48), cols]),
            push(ga.at[own, cols], ga.at[own, cols], (pt, ph), ga.at[rows(48 * ph, 48), cols]),
            push(oth.at[:, cols], ga.at[own, cols], (pt, pho), ga.at[rows(48 * pho, 48), cols]),
        ]

    def slab_one(lo, hi):
        cols = pl.ds(lo, hi - lo)
        piece = lax.rem(h, 4)
        whole = ga.at[own, cols]
        waits = []
        for src, peer, row in (
            (oth.at[:, cols], sib, hs),
            (whole, (pt, ph), ph),
            (oth.at[:, cols], (pt, pho), pho),
        ):
            copy = remote(src, whole, peer, index())
            pl.when(piece == x)(copy.start)
            started.append(lambda copy=copy: pl.when(piece == x)(copy.wait_send))
            landed = ga.at[rows(48 * row, 48), cols]
            arrival = remote(landed, landed, peer, used[0] - 1)
            waits.append(
                lambda arrival=arrival, row=row: pl.when(lax.rem(row, 4) == x)(arrival.wait_recv)
            )
        slab_waits[lo] = waits

    def slab_wait(lo):
        for wait in slab_waits[lo]:
            wait()

    def slot(step):
        return 192 * lax.rem(z + step + 8, 8)

    def ring_z(lo, hi, forward):
        cols = pl.ds(lo, hi - lo)
        slab_wait(lo)
        for s in range(4):
            a, n, b = (0, 192, 0) if s < 3 else (0, 96, 96)

            def view(step, base):
                return ga.at[rows(slot(step) + base, n), cols]

            up = push(view(-s, a), view(-s, a), zup, view(-s - 1, a))
            dn = push(view(s, b), view(s, b), zdn, view(s + 1, b))
            yield
            up()
            dn()
        yield from finish(lo, hi, forward)

    def finish(lo, hi, forward):
        if forward:
            cols, there = pl.ds(lo, hi - lo), pl.ds(lo - SO0, hi - lo)
            wait = push(ga.at[:, cols], gb.at[:, there], sib, gb.at[:, there])
            yield
            wait()

    def ring_x(lo, hi, forward):
        cols = pl.ds(lo, hi - lo)
        slab_wait(lo)

        def piece(step, quarter):
            return ga.at[rows(slot(step) + 48 * quarter, 48), cols]

        fan_up, fan_dn = index(), index()

        def spread(*steps):
            for step in steps:
                part = piece(step, x)
                remote(part, part, xup, fan_up).start()
                remote(part, part, xdn, fan_dn).start()

        def gathered(peer, i, count):
            whole = ga.at[pl.ds(0, 48 * count), cols]
            copy = remote(whole, whole, peer, i)
            started.append(copy.wait_send)
            return copy.wait_recv

        spread(0)
        for s in range(4):
            up = push(piece(-s, x), piece(-s, x), zup, piece(-s - 1, x))
            dn = None
            if s < 3:
                dn = push(piece(s, x), piece(s, x), zdn, piece(s + 1, x))
            yield
            up()
            if s < 3:
                dn()
                spread(-s - 1, s + 1)
            else:
                spread(-s - 1)
        to_up = gathered(xup, fan_up, 8)
        to_dn = gathered(xdn, fan_dn, 8)
        left, right = lax.rem(x + 3, 4), lax.rem(x + 1, 4)

        def fan(quarter, slabs, peer):
            i = index()

            def one(k, carry):
                part = piece(k, quarter)
                remote(part, part, peer, i).start()
                return carry

            lax.fori_loop(slabs[0], slabs[1], one, 0)
            return gathered(peer, i, slabs[1] - slabs[0])

        yield
        to_up()
        to_dn()
        to_up = fan(left, (0, 4), xup)
        to_dn = fan(right, (4, 8), xdn)
        yield
        to_up()
        to_dn()
        yield from finish(lo, hi, forward)

    def send_latent(place, src, peer):
        got_latent[place] = push(src, lats.at[place], peer, lats.at[place])

    got_latent = {}
    slab(K0, V0)
    slab_one(Q0, SO0)
    slab_one(CO0, END)
    slab(V0, Q0)
    send_latent(0, lat_in, flip)
    send_latent(3, lat_in, at(0, edge))

    rings = {
        "k": ring_z(K0, V0, False),
        "v": ring_z(V0, Q0, False),
        "q": ring_x(Q0, SO0, False),
        "so": ring_z(SO0, CQ0, True),
        "cq": ring_x(CQ0, CO0, True),
        "co": ring_x(CO0, END, True),
    }

    def pump(*names):
        for name in names:
            next(rings[name], None)

    def drain(*names):
        for name in names:
            for _ in rings[name]:
                pass

    pump("k", "q", "co", "v")

    near, far = 2 - 2 * ylo, 2 * ylo
    places = [(near, 1), (far, 1), (near, 0), (1, 0), (far, 0), (1, 1)]
    shown = [(f, 1 + c if own_row else 3 * c) for f, own_row in places]
    hidden = [(f, 2 - c if own_row else 3 - 3 * c) for f, own_row in places]
    got_mod = {}

    def modulate(place, src):
        f, r = shown[place]
        here = modb.at[f, rows(TOK * r, TOK)]
        values = layer_norm(src[...].astype(F32)) * (1.0 + mod[1:2, :]) + mod[0:1, :]
        here[...] = values.astype(BF)
        f, r = hidden[place]
        got_mod[place] = push(here, here, sib, modb.at[f, rows(TOK * r, TOK)])

    def modulate_halo(place):
        modulate(place, lats.at[place])

    loads[1].wait()
    modulate(5, lat)

    loads[2].wait()
    loads[3].wait()
    txt[...] = dot_nt(wt[...], ts[...]).astype(BF)
    mine = pl.ds(pl.multiple_of(256 * c, 128), 256)
    pl.when(lax.rem(h, 4) == x)(lambda mine=mine: keep(TX0, txt[:, mine]))
    oth[:, pl.ds(TX0, 256)] = txt[:, pl.ds(pl.multiple_of(256 * (1 - c), 128), 256)]
    slab_one(CQ0, CO0)
    pump("cq")
    pump("k", "q", "co", "v")

    lane = lax.broadcasted_iota(jnp.int32, (8, WIN), 1)
    frame = lax.broadcasted_iota(jnp.int32, (8, WIN), 0)

    def step_of(value, *edges):
        total = jnp.zeros_like(value)
        for mark_at in edges:
            total = total + (value >= mark_at).astype(jnp.int32)
        return total

    row_at = step_of(lane, 208, 416)
    within = lane - 208 * row_at
    within = within - 104 * step_of(within, 104)
    code = jnp.where(lane < 624, 12 * frame + 4 * row_at + step_of(within, 26, 52, 78), -2)
    for q in range(4):
        allowed = code == 16 + q
        for j in range(8):
            dt, dr, dc = off[0, 0, 0, q, j], off[1, 0, 0, q, j], off[2, 0, 0, q, j]
            ft, rt, ct = t + dt, h + dr, q + dc
            usable = (ft >= 0) & (ft < 8) & (rt >= 0) & (rt < 32) & (ct >= 0) & (ct < 4)
            target = jnp.where(usable, 12 * (dt + 1) + 4 * (dr + 1) + ct, -1)
            allowed = allowed | (code == target)
        rb[c, pl.ds(8 * q, 8), :] = jnp.where(allowed, 0.0, -jnp.inf).astype(F32)
    got_rb = push(rb.at[c], rb.at[c], sib, rb.at[1 - c])
    got_rb()
    token = lax.broadcasted_iota(jnp.int32, (TOK, 1), 0)
    token = token - 104 * step_of(token, 104)
    tile = step_of(token, 26, 52, 78)

    def masks(i, carry):
        r, f = lax.div(i, 3), lax.rem(i, 3)
        picked = rb[r, pl.ds(f, 1), :]
        for q in range(1, 4):
            picked = jnp.where(tile == q, rb[r, pl.ds(8 * q + f, 1), :], picked)
        mb[r, f] = jnp.broadcast_to(picked, (TOK, WIN))
        return carry

    lax.fori_loop(0, 6, masks, 0)
    for f in range(3):
        kvb[f, pl.ds(832, 16), :] = jnp.zeros((16, 768), BF)
    pump("cq")
    got_latent[0]()
    send_latent(1, lats.at[0], beyond)
    pump("k", "q", "co", "v", "cq")

    def gain(i, half):
        return ng[i : i + 1, pl.ds(pl.multiple_of(HALF * half, 128), HALF)]

    def squares(values, mine_at, theirs_at):
        total = jnp.sum(values * values, axis=-1, keepdims=True)
        mine_at[...] = jnp.broadcast_to(total, mine_at.shape)
        return push(mine_at, theirs_at, sib, theirs_at)

    def inverse_rms(mine_at, theirs_at):
        total = mine_at[:, 0:1] + theirs_at[:, 0:1]
        return lax.rsqrt(total * (1.0 / 768) + 1e-06)

    got_squares = {}

    def keys_values(name, f, r, n):
        here, flat = pl.ds(TOK * r, TOK * n), rows(TOK * (4 * f + r), TOK * n)
        modulated = modb[f, here, :]
        keys = dot(modulated, ga[:, pl.ds(K0, HALF)])
        kraw[flat, :] = keys
        got_squares[name] = squares(keys, ssb.at[0, flat], ssb.at[1, flat])
        kvb[f, here, pl.ds(HALF, HALF)] = dot(modulated, ga[:, pl.ds(V0, HALF)]).astype(BF)

    def normal_keys(name, f, r, n):
        here, flat = pl.ds(TOK * r, TOK * n), rows(TOK * (4 * f + r), TOK * n)
        got_squares[name]()
        scaled = kraw[flat, :] * inverse_rms(ssb.at[0, flat], ssb.at[1, flat])
        kvb[f, here, pl.ds(0, HALF)] = (scaled * gain(1, c)).astype(BF)

    both = pl.ds(TOK, 2 * TOK)
    got_queries = []

    def queries():
        raw[...] = dot(modb[1, both, :], ga[:, pl.ds(Q0, HALF)])
        got_queries.append(squares(raw[...], ssq.at[0], ssq.at[1]))

    def normal_queries():
        got_queries[0]()
        qb[...] = (raw[...] * inverse_rms(ssq.at[0], ssq.at[1]) * (gain(0, c) * SCALE)).astype(BF)

    modulate_halo(0)
    got_latent[3]()
    send_latent(2, lats.at[3], flip)
    send_latent(4, lats.at[3], outer)
    pump("k", "q", "co", "v", "cq")
    slab(SO0, CQ0)
    modulate_halo(3)
    drain("k", "v")
    pump("so", "q", "co", "cq")
    got_mod[5]()
    keys_values("own", 1, 1, 2)
    pump("so")
    got_mod[0]()
    keys_values("near", near, 1, 2)
    normal_keys("own", 1, 1, 2)
    pump("q", "co", "cq")
    got_latent[1]()
    modulate_halo(1)
    normal_keys("near", near, 1, 2)
    drain("q")
    queries()
    pump("so", "co", "cq")
    got_mod[3]()
    keys_values("edge0", 1, 0, 1)
    keys_values("edge3", 1, 3, 1)
    normal_queries()
    got_mod[1]()
    keys_values("far", far, 1, 2)
    normal_keys("edge0", 1, 0, 1)
    normal_keys("edge3", 1, 3, 1)
    pump("so", "co", "cq")
    got_latent[2]()
    modulate_halo(2)
    normal_keys("far", far, 1, 2)
    got_latent[4]()
    modulate_halo(4)
    got_mod[2]()
    keys_values("near0", near, 0, 1)
    keys_values("near3", near, 3, 1)
    got_mod[4]()
    keys_values("far0", far, 0, 1)
    keys_values("far3", far, 3, 1)
    normal_keys("near0", near, 0, 1)
    normal_keys("near3", near, 3, 1)
    pump("so")
    normal_keys("far0", far, 0, 1)
    normal_keys("far3", far, 3, 1)

    def attend(r, i):
        q = qb[pl.ds(TOK * r, TOK), pl.ds(128 * i, 128)]
        keys = pl.ds(TOK * r, WIN)
        scores = [dot_nt(q, kvb[f, keys, pl.ds(128 * i, 128)]) + mb[r, f] for f in range(3)]
        largest = jnp.max(scores[0], axis=-1, keepdims=True)
        for s in scores[1:]:
            largest = jnp.maximum(largest, jnp.max(s, axis=-1, keepdims=True))
        total, mixed = 0.0, 0.0
        for f in range(3):
            p = jnp.exp2(scores[f] - largest)
            total = total + jnp.sum(p, axis=-1, keepdims=True)
            mixed = mixed + dot(p.astype(BF), kvb[f, keys, pl.ds(HALF + 128 * i, 128)])
        mixb[pl.ds(TOK * r, TOK), pl.ds(128 * i, 128)] = (mixed / total).astype(BF)

    for r in range(2):
        for i in range(3):
            attend(r, i)
            pump("cq", "co", "so")
    mine = rows(TOK * c, TOK)
    theirs = rows(TOK * (1 - c), TOK)
    got_mix = push(mixb.at[theirs, :], mixo, sib, mixo)
    drain("so")
    got_mix()

    def outward(mine_in, other_in, lo, i):
        n = pl.ds(pl.multiple_of(256 * i, 256), 256)
        return dot_nt(mine_in, ga[n, pl.ds(lo, HALF)]) + dot_nt(
            other_in, gb[n, pl.ds(lo - SO0, HALF)]
        )

    mix_mine, mix_other = mixb[mine, :], mixo[...]

    def self_out(i, carry):
        n = pl.ds(pl.multiple_of(256 * i, 256), 256)
        res[:, n] = lat[:, n].astype(F32) + mod[2:3, n] * outward(mix_mine, mix_other, SO0, i)
        return carry

    lax.fori_loop(0, 6, self_out, 0)
    drain("cq")
    normed = (layer_norm(res[...]) * cn[0:1, :] + cn[1:2, :]).astype(BF)
    cq_mine = dot(normed, ga[:, pl.ds(CQ0, HALF)])
    cq_other = dot(normed, gb[:, pl.ds(CQ0 - SO0, HALF)])
    square = jnp.sum(cq_mine * cq_mine, axis=-1, keepdims=True)
    square = square + jnp.sum(cq_other * cq_other, axis=-1, keepdims=True)
    inverse = lax.rsqrt(square * (1.0 / 768) + 1e-06) * SCALE
    raw[0:TOK, :] = cq_mine * inverse * (gain(2, c) * gain(3, c))
    raw[TOK : 2 * TOK, :] = cq_other * inverse * (gain(2, 1 - c) * gain(3, 1 - c))

    def text_scale(ref, lo):
        keys = ref[0:768, pl.ds(lo, 256)].astype(F32)
        return lax.rsqrt(jnp.sum(keys * keys, axis=0, keepdims=True) * (1.0 / 768) + 1e-06)

    real = [
        tmask[:, pl.ds(pl.multiple_of(256 * half, 128), 256)] == 1 for half in (c, 1 - c)
    ]
    parts = [(ga, TX0), (gb, TX0 - SO0)]
    scales = [text_scale(*part) for part in parts]
    for k in range(2):
        base = HALF * c if k == 0 else HALF * (1 - c)
        for i in range(3):
            q = raw[pl.ds(TOK * k, TOK), pl.ds(128 * i, 128)].astype(BF)
            krow, vrow = rows(base + 128 * i, 128), rows(768 + base + 128 * i, 128)
            scores = [
                jnp.where(real[j], dot(q, ref[krow, pl.ds(lo, 256)]) * scales[j], -jnp.inf)
                for j, (ref, lo) in enumerate(parts)
            ]
            largest = jnp.maximum(
                jnp.max(scores[0], axis=-1, keepdims=True),
                jnp.max(scores[1], axis=-1, keepdims=True),
            )
            total, mixed = 0.0, 0.0
            for j, (ref, lo) in enumerate(parts):
                p = jnp.exp2(scores[j] - largest)
                total = total + jnp.sum(p, axis=-1, keepdims=True)
                mixed = mixed + dot_nt(p.astype(BF), ref[vrow, pl.ds(lo, 256)])
            qb[pl.ds(TOK * k, TOK), pl.ds(128 * i, 128)] = (mixed / total).astype(BF)
    drain("co")
    cross_mine, cross_other = qb[0:TOK, :], qb[TOK : 2 * TOK, :]

    def cross_out(i, carry):
        n = pl.ds(pl.multiple_of(256 * i, 256), 256)
        out[:, n] = (res[:, n] + outward(cross_mine, cross_other, CO0, i)).astype(BF)
        return carry

    lax.fori_loop(0, 6, cross_out, 0)
    assert used[0] <= NSEM
    for wait in started:
        wait()


def body(
    latent, modulation, cross_norm, norm_gains, w_main, text_states, w_text, tile_offsets, text_mask
):
    vmem = pl.BlockSpec(memory_space=pltpu.VMEM)
    smem = pl.BlockSpec(memory_space=pltpu.SMEM)
    hbm = pl.BlockSpec(memory_space=pl.ANY)
    result = pl.pallas_call(
        kernel,
        out_shape=jax.ShapeDtypeStruct((TOK, D), BF),
        in_specs=[hbm, vmem, vmem, vmem, hbm, hbm, hbm, smem, vmem],
        out_specs=vmem,
        scratch_shapes=[
            pltpu.VMEM((TOK, D), BF),
            pltpu.VMEM((48, 4608), BF),
            pltpu.VMEM((512, D), BF),
            pltpu.VMEM((48, D), BF),
            pltpu.VMEM((D, END), BF),
            pltpu.VMEM((D, END - SO0), BF),
            pltpu.VMEM((48, END), BF),
            pltpu.VMEM((3, 4 * TOK, D), BF),
            pltpu.VMEM((5, TOK, D), BF),
            pltpu.VMEM((3, 848, 768), BF),
            pltpu.VMEM((12 * TOK, HALF), F32),
            pltpu.VMEM((2, 12 * TOK, 128), F32),
            pltpu.VMEM((2 * TOK, HALF), F32),
            pltpu.VMEM((2, 2 * TOK, 128), F32),
            pltpu.VMEM((2 * TOK, HALF), BF),
            pltpu.VMEM((2, 32, WIN), F32),
            pltpu.VMEM((2, 3, TOK, WIN), F32),
            pltpu.VMEM((2 * TOK, HALF), BF),
            pltpu.VMEM((TOK, HALF), BF),
            pltpu.VMEM((TOK, D), F32),
            pltpu.VMEM((48, 512), BF),
            pltpu.SemaphoreType.DMA((NSEM,)),
            pltpu.SemaphoreType.DMA((NSEM,)),
            pltpu.SemaphoreType.DMA((4,)),
        ],
        compiler_params=pltpu.CompilerParams(
            collective_id=0, has_side_effects=True, vmem_limit_bytes=60 * 1024 * 1024
        ),
        cost_estimate=pl.CostEstimate(
            flops=6_000_000_000, bytes_accessed=6_000_000, transcendentals=3_000_000
        ),
    )(
        latent.reshape(TOK, D),
        modulation,
        cross_norm,
        norm_gains,
        w_main,
        text_states,
        w_text.T,
        tile_offsets,
        text_mask.reshape(1, 512),
    )
    return result.reshape(latent.shape)


def solution(mesh):
    placed = (
        P("tm", "height", None, None),
        P(),
        P(),
        P(),
        P("height", None),
        P(),
        P(None, "height"),
        P(None, "tm", "height", None, None),
        P(),
    )
    return jax.shard_map(
        body, mesh=mesh, in_specs=placed, out_specs=P("tm", "height", None, None), check_vma=False
    )
```

```python
import jax
import jax.numpy as jnp
from jax import lax
from jax.experimental import pallas as pl
from jax.experimental.pallas import tpu as pltpu
from jax.sharding import PartitionSpec as P

MESH = pl.DeviceIdType.MESH
BF = jnp.bfloat16
F32 = jnp.float32
TOK = 208
WIN = 640
HALF = 384
D = 1536
SCALE = 128.0**-0.5 * 1.4426950408889634
K0, V0, Q0, SO0, CQ0, TX0, CO0, END = 0, 384, 768, 1152, 1536, 1920, 2176, 2560
NSEM = 160
LAG = 0


def layer_norm(values):
    average = jnp.mean(values, axis=-1, keepdims=True)
    centred = values - average
    variance = jnp.mean(centred * centred, axis=-1, keepdims=True)
    return centred * lax.rsqrt(variance + 1e-06)


def dot_nt(a, b):
    return lax.dot_general(a, b, (((1,), (1,)), ((), ())), preferred_element_type=F32)


def dot(a, b):
    return jnp.dot(a, b, preferred_element_type=F32)


def kernel(
    lat_in, mod, cn, ng, w_in, ts_in, wt_in, off, tmask, out,
    lat, w, ts, wt, ga, gb, oth, modb, lats, kvb, kraw, ssb, raw, ssq, qb, rb, mb, mixb, mixo, res, txt,
    send, recv, load,
):
    t = lax.axis_index("tm")
    h = lax.axis_index("height")
    c = lax.rem(h, 2)
    yhi = lax.rem(lax.div(h, 2), 2)
    z = lax.div(h, 4)
    x = lax.div(t, 2)
    ylo = lax.rem(t, 2)

    loads = [
        pltpu.make_async_copy(src, dst, load.at[i])
        for i, (src, dst) in enumerate(((w_in, w), (lat_in, lat), (wt_in, wt), (ts_in, ts)))
    ]
    for copy in loads:
        copy.start()

    def at(dt, dh):
        return (lax.rem(t + dt + 8, 8), lax.rem(h + dh + 32, 32))

    hs = h + 1 - 2 * c
    sib = (t, hs)
    pt, ph = t + 1 - 2 * ylo, h + 2 - 4 * yhi
    pho = ph + 1 - 2 * c
    zup, zdn, xup, xdn = at(0, 4), at(0, -4), at(2, 0), at(-2, 0)
    edge = 2 * c - 1
    flip, outer, beyond = at(1 - 2 * ylo, 0), at(2 * ylo - 1, 0), at(2 - 4 * ylo, 0)
    peers = [sib, (pt, ph), (pt, pho), zup, zdn, xup, xdn, flip, outer, at(0, edge)]

    barrier = pltpu.get_barrier_semaphore()
    for peer in peers:
        pl.semaphore_signal(barrier, inc=1, device_id=peer, device_id_type=MESH)

    def rows(start, count):
        return pl.ds(pl.multiple_of(start, 16), count)

    own = rows(48 * h, 48)

    def keep(col, values):
        ga[own, pl.ds(col, values.shape[1])] = values

    loads[0].wait()
    for part, col in ((1, K0), (2, V0), (0, Q0), (4, SO0), (3, CQ0), (5, CO0)):
        mine = pl.ds(pl.multiple_of(768 * part + HALF * c, 128), HALF)
        other = pl.ds(pl.multiple_of(768 * part + HALF * (1 - c), 128), HALF)
        oth[:, pl.ds(col, HALF)] = w[:, other]
        if col in (K0, V0, SO0, CO0):
            ga[own, pl.ds(col, HALF)] = w[:, mine]
        else:
            pl.when(lax.rem(h, 4) == x)(lambda col=col, mine=mine: keep(col, w[:, mine]))
    pl.semaphore_wait(barrier, len(peers))

    used = [0]
    started = []

    def index():
        used[0] += 1
        return used[0] - 1

    def remote(src, dst, peer, i):
        return pltpu.make_async_remote_copy(
            src_ref=src, dst_ref=dst, send_sem=send.at[i], recv_sem=recv.at[i],
            device_id=peer, device_id_type=MESH,
        )

    def push(src, dst, peer, arriving):
        i = index()
        copy = remote(src, dst, peer, i)
        copy.start()
        started.append(copy.wait_send)
        return remote(arriving, arriving, peer, i).wait_recv

    slab_waits = {}

    def slab(lo, hi):
        cols = pl.ds(lo, hi - lo)
        slab_waits[lo] = [
            push(oth.at[:, cols], ga.at[own, cols], sib, ga.at[rows(48 * hs, 48), cols]),
            push(ga.at[own, cols], ga.at[own, cols], (pt, ph), ga.at[rows(48 * ph, 48), cols]),
            push(oth.at[:, cols], ga.at[own, cols], (pt, pho), ga.at[rows(48 * pho, 48), cols]),
        ]

    def slab_one(lo, hi):
        cols = pl.ds(lo, hi - lo)
        piece = lax.rem(h, 4)
        whole = ga.at[own, cols]
        waits = []
        for src, peer, row in (
            (oth.at[:, cols], sib, hs),
            (whole, (pt, ph), ph),
            (oth.at[:, cols], (pt, pho), pho),
        ):
            copy = remote(src, whole, peer, index())
            pl.when(piece == x)(copy.start)
            started.append(lambda copy=copy: pl.when(piece == x)(copy.wait_send))
            landed = ga.at[rows(48 * row, 48), cols]
            arrival = remote(landed, landed, peer, used[0] - 1)
            waits.append(
                lambda arrival=arrival, row=row: pl.when(lax.rem(row, 4) == x)(arrival.wait_recv)
            )
        slab_waits[lo] = waits

    def slab_wait(lo):
        for wait in slab_waits[lo]:
            wait()

    def slot(step):
        return 192 * lax.rem(z + step + 8, 8)

    def ring_z(lo, hi, forward):
        cols = pl.ds(lo, hi - lo)
        slab_wait(lo)
        for s in range(4):
            a, n, b = (0, 192, 0) if s < 3 else (0, 96, 96)

            def view(step, base):
                return ga.at[rows(slot(step) + base, n), cols]

            up = push(view(-s, a), view(-s, a), zup, view(-s - 1, a))
            dn = push(view(s, b), view(s, b), zdn, view(s + 1, b))
            yield
            up()
            dn()
        yield from finish(lo, hi, forward)

    def finish(lo, hi, forward):
        if forward:
            cols, there = pl.ds(lo, hi - lo), pl.ds(lo - SO0, hi - lo)
            wait = push(ga.at[:, cols], gb.at[:, there], sib, gb.at[:, there])
            yield
            wait()

    def ring_x(lo, hi, forward):
        cols = pl.ds(lo, hi - lo)
        slab_wait(lo)

        def piece(step, quarter):
            return ga.at[rows(slot(step) + 48 * quarter, 48), cols]

        left, right = lax.rem(x + 3, 4), lax.rem(x + 1, 4)
        last_up, last_dn = index(), index()

        def gathered(peer, i, count):
            whole = ga.at[pl.ds(0, 48 * count), cols]
            copy = remote(whole, whole, peer, i)
            started.append(copy.wait_send)
            return copy.wait_recv

        def beside(*steps):
            i, j = index(), index()
            for step in steps:
                part = piece(step, x)
                remote(part, part, xup, i).start()
                remote(part, part, xdn, j).start()
            return steps, gathered(xup, i, len(steps)), gathered(xdn, j, len(steps))

        def pass_on(steps, from_left, from_right):
            from_left()
            from_right()
            if steps[0] != -4:
                part = piece(steps[0], left)
                remote(part, part, xup, last_up).start()
            if steps[-1] != 0:
                part = piece(steps[-1], right)
                remote(part, part, xdn, last_dn).start()

        def along(s):
            waits = [push(piece(-s, x), piece(-s, x), zup, piece(-s - 1, x))]
            if s < 3:
                waits.append(push(piece(s, x), piece(s, x), zdn, piece(s + 1, x)))
            return waits

        waits, held = along(0), [beside(0)]
        for s in range(1, 5):
            yield
            for wait in waits:
                wait()
            if s < 4:
                waits = along(s)
                held.append(beside(-s, s))
            else:
                held.append(beside(-s))
            if s > LAG:
                pass_on(*held.pop(0))
        while held:
            yield
            pass_on(*held.pop(0))
        to_up, to_dn = gathered(xup, last_up, 4), gathered(xdn, last_dn, 4)
        yield
        to_up()
        to_dn()
        yield from finish(lo, hi, forward)

    def send_latent(place, src, peer):
        got_latent[place] = push(src, lats.at[place], peer, lats.at[place])

    got_latent = {}
    slab(K0, V0)
    slab_one(Q0, SO0)
    slab(V0, Q0)
    send_latent(0, lat_in, flip)
    slab(SO0, CQ0)

    rings = {
        "k": ring_z(K0, V0, False),
        "v": ring_z(V0, Q0, False),
        "q": ring_x(Q0, SO0, False),
        "so": ring_z(SO0, CQ0, True),
        "cq": ring_x(CQ0, CO0, True),
        "co": ring_z(CO0, END, True),
    }

    def pump(*names):
        for name in names:
            next(rings[name], None)

    def drain(*names):
        for name in names:
            for _ in rings[name]:
                pass

    pump("q", "k", "v")

    near, far = 2 - 2 * ylo, 2 * ylo
    places = [(near, 1), (far, 1), (near, 0), (1, 0), (far, 0), (1, 1)]
    shown = [(f, 1 + c if own_row else 3 * c) for f, own_row in places]
    hidden = [(f, 2 - c if own_row else 3 - 3 * c) for f, own_row in places]
    got_mod = {}

    def modulate(place, src):
        f, r = shown[place]
        here = modb.at[f, rows(TOK * r, TOK)]
        values = layer_norm(src[...].astype(F32)) * (1.0 + mod[1:2, :]) + mod[0:1, :]
        here[...] = values.astype(BF)
        f, r = hidden[place]
        got_mod[place] = push(here, here, sib, modb.at[f, rows(TOK * r, TOK)])

    def modulate_halo(place):
        modulate(place, lats.at[place])

    loads[1].wait()
    modulate(5, lat)

    loads[2].wait()
    loads[3].wait()
    txt[...] = dot_nt(wt[...], ts[...]).astype(BF)
    mine = pl.ds(pl.multiple_of(256 * c, 128), 256)
    pl.when(lax.rem(h, 4) == x)(lambda mine=mine: keep(TX0, txt[:, mine]))
    oth[:, pl.ds(TX0, 256)] = txt[:, pl.ds(pl.multiple_of(256 * (1 - c), 128), 256)]
    slab_one(CQ0, CO0)
    slab(CO0, END)
    pump("cq")
    send_latent(3, lat_in, at(0, edge))

    lane = lax.broadcasted_iota(jnp.int32, (8, WIN), 1)
    frame = lax.broadcasted_iota(jnp.int32, (8, WIN), 0)

    def step_of(value, *edges):
        total = jnp.zeros_like(value)
        for mark_at in edges:
            total = total + (value >= mark_at).astype(jnp.int32)
        return total

    row_at = step_of(lane, 208, 416)
    within = lane - 208 * row_at
    within = within - 104 * step_of(within, 104)
    code = jnp.where(lane < 624, 12 * frame + 4 * row_at + step_of(within, 26, 52, 78), -2)
    for q in range(4):
        allowed = code == 16 + q
        for j in range(8):
            dt, dr, dc = off[0, 0, 0, q, j], off[1, 0, 0, q, j], off[2, 0, 0, q, j]
            ft, rt, ct = t + dt, h + dr, q + dc
            usable = (ft >= 0) & (ft < 8) & (rt >= 0) & (rt < 32) & (ct >= 0) & (ct < 4)
            target = jnp.where(usable, 12 * (dt + 1) + 4 * (dr + 1) + ct, -1)
            allowed = allowed | (code == target)
        rb[c, pl.ds(8 * q, 8), :] = jnp.where(allowed, 0.0, -jnp.inf).astype(F32)
    got_rb = push(rb.at[c], rb.at[c], sib, rb.at[1 - c])
    got_rb()
    token = lax.broadcasted_iota(jnp.int32, (TOK, 1), 0)
    token = token - 104 * step_of(token, 104)
    tile = step_of(token, 26, 52, 78)

    def masks(i, carry):
        r, f = lax.div(i, 3), lax.rem(i, 3)
        picked = rb[r, pl.ds(f, 1), :]
        for q in range(1, 4):
            picked = jnp.where(tile == q, rb[r, pl.ds(8 * q + f, 1), :], picked)
        mb[r, f] = jnp.broadcast_to(picked, (TOK, WIN))
        return carry

    lax.fori_loop(0, 6, masks, 0)
    for f in range(3):
        kvb[f, pl.ds(832, 16), :] = jnp.zeros((16, 768), BF)
    pump("k", "q", "v", "cq")
    got_latent[0]()
    send_latent(1, lats.at[0], beyond)
    pump("k", "q", "v", "cq")

    def gain(i, half):
        return ng[i : i + 1, pl.ds(pl.multiple_of(HALF * half, 128), HALF)]

    def squares(values, mine_at, theirs_at):
        total = jnp.sum(values * values, axis=-1, keepdims=True)
        mine_at[...] = jnp.broadcast_to(total, mine_at.shape)
        return push(mine_at, theirs_at, sib, theirs_at)

    def inverse_rms(mine_at, theirs_at):
        total = mine_at[:, 0:1] + theirs_at[:, 0:1]
        return lax.rsqrt(total * (1.0 / 768) + 1e-06)

    got_squares = {}

    def keys_values(name, f, r, n):
        here, flat = pl.ds(TOK * r, TOK * n), rows(TOK * (4 * f + r), TOK * n)
        modulated = modb[f, here, :]
        keys = dot(modulated, ga[:, pl.ds(K0, HALF)])
        kraw[flat, :] = keys
        got_squares[name] = squares(keys, ssb.at[0, flat], ssb.at[1, flat])
        kvb[f, here, pl.ds(HALF, HALF)] = dot(modulated, ga[:, pl.ds(V0, HALF)]).astype(BF)

    def normal_keys(name, f, r, n):
        here, flat = pl.ds(TOK * r, TOK * n), rows(TOK * (4 * f + r), TOK * n)
        got_squares[name]()
        scaled = kraw[flat, :] * inverse_rms(ssb.at[0, flat], ssb.at[1, flat])
        kvb[f, here, pl.ds(0, HALF)] = (scaled * gain(1, c)).astype(BF)

    both = pl.ds(TOK, 2 * TOK)
    got_queries = []

    def queries():
        raw[...] = dot(modb[1, both, :], ga[:, pl.ds(Q0, HALF)])
        got_queries.append(squares(raw[...], ssq.at[0], ssq.at[1]))

    def normal_queries():
        got_queries[0]()
        qb[...] = (raw[...] * inverse_rms(ssq.at[0], ssq.at[1]) * (gain(0, c) * SCALE)).astype(BF)

    modulate_halo(0)
    got_latent[3]()
    send_latent(2, lats.at[3], flip)
    send_latent(4, lats.at[3], outer)
    pump("k", "q", "v", "cq")
    modulate_halo(3)
    drain("k", "v")
    pump("so", "q", "co", "cq")
    got_mod[5]()
    keys_values("own", 1, 1, 2)
    pump("so")
    got_mod[0]()
    keys_values("near", near, 1, 2)
    normal_keys("own", 1, 1, 2)
    pump("q", "co", "cq")
    got_latent[1]()
    modulate_halo(1)
    normal_keys("near", near, 1, 2)
    drain("q")
    queries()
    pump("so", "co", "cq")
    got_mod[3]()
    keys_values("edge0", 1, 0, 1)
    keys_values("edge3", 1, 3, 1)
    normal_queries()
    got_mod[1]()
    keys_values("far", far, 1, 2)
    normal_keys("edge0", 1, 0, 1)
    normal_keys("edge3", 1, 3, 1)
    pump("so", "co", "cq")
    got_latent[2]()
    modulate_halo(2)
    normal_keys("far", far, 1, 2)
    got_latent[4]()
    modulate_halo(4)
    got_mod[2]()
    keys_values("near0", near, 0, 1)
    keys_values("near3", near, 3, 1)
    got_mod[4]()
    keys_values("far0", far, 0, 1)
    keys_values("far3", far, 3, 1)
    normal_keys("near0", near, 0, 1)
    normal_keys("near3", near, 3, 1)
    pump("so")
    normal_keys("far0", far, 0, 1)
    normal_keys("far3", far, 3, 1)

    def attend(r, i):
        q = qb[pl.ds(TOK * r, TOK), pl.ds(128 * i, 128)]
        keys = pl.ds(TOK * r, WIN)
        scores = [dot_nt(q, kvb[f, keys, pl.ds(128 * i, 128)]) + mb[r, f] for f in range(3)]
        largest = jnp.max(scores[0], axis=-1, keepdims=True)
        for s in scores[1:]:
            largest = jnp.maximum(largest, jnp.max(s, axis=-1, keepdims=True))
        total, mixed = 0.0, 0.0
        for f in range(3):
            p = jnp.exp2(scores[f] - largest)
            total = total + jnp.sum(p, axis=-1, keepdims=True)
            mixed = mixed + dot(p.astype(BF), kvb[f, keys, pl.ds(HALF + 128 * i, 128)])
        mixb[pl.ds(TOK * r, TOK), pl.ds(128 * i, 128)] = (mixed / total).astype(BF)

    for r in range(2):
        for i in range(3):
            attend(r, i)
            pump("cq", "co", "so")
    mine = rows(TOK * c, TOK)
    theirs = rows(TOK * (1 - c), TOK)
    got_mix = push(mixb.at[theirs, :], mixo, sib, mixo)
    drain("so")
    got_mix()

    def outward(mine_in, other_in, lo, i):
        n = pl.ds(pl.multiple_of(256 * i, 256), 256)
        return dot_nt(mine_in, ga[n, pl.ds(lo, HALF)]) + dot_nt(
            other_in, gb[n, pl.ds(lo - SO0, HALF)]
        )

    mix_mine, mix_other = mixb[mine, :], mixo[...]

    def self_out(i, carry):
        n = pl.ds(pl.multiple_of(256 * i, 256), 256)
        res[:, n] = lat[:, n].astype(F32) + mod[2:3, n] * outward(mix_mine, mix_other, SO0, i)
        return carry

    lax.fori_loop(0, 6, self_out, 0)
    drain("cq")
    normed = (layer_norm(res[...]) * cn[0:1, :] + cn[1:2, :]).astype(BF)
    cq_mine = dot(normed, ga[:, pl.ds(CQ0, HALF)])
    cq_other = dot(normed, gb[:, pl.ds(CQ0 - SO0, HALF)])
    square = jnp.sum(cq_mine * cq_mine, axis=-1, keepdims=True)
    square = square + jnp.sum(cq_other * cq_other, axis=-1, keepdims=True)
    inverse = lax.rsqrt(square * (1.0 / 768) + 1e-06) * SCALE
    raw[0:TOK, :] = cq_mine * inverse * (gain(2, c) * gain(3, c))
    raw[TOK : 2 * TOK, :] = cq_other * inverse * (gain(2, 1 - c) * gain(3, 1 - c))

    def text_scale(ref, lo):
        keys = ref[0:768, pl.ds(lo, 256)].astype(F32)
        return lax.rsqrt(jnp.sum(keys * keys, axis=0, keepdims=True) * (1.0 / 768) + 1e-06)

    real = [
        tmask[:, pl.ds(pl.multiple_of(256 * half, 128), 256)] == 1 for half in (c, 1 - c)
    ]
    parts = [(ga, TX0), (gb, TX0 - SO0)]
    scales = [text_scale(*part) for part in parts]
    for k in range(2):
        base = HALF * c if k == 0 else HALF * (1 - c)
        for i in range(3):
            q = raw[pl.ds(TOK * k, TOK), pl.ds(128 * i, 128)].astype(BF)
            krow, vrow = rows(base + 128 * i, 128), rows(768 + base + 128 * i, 128)
            scores = [
                jnp.where(real[j], dot(q, ref[krow, pl.ds(lo, 256)]) * scales[j], -jnp.inf)
                for j, (ref, lo) in enumerate(parts)
            ]
            largest = jnp.maximum(
                jnp.max(scores[0], axis=-1, keepdims=True),
                jnp.max(scores[1], axis=-1, keepdims=True),
            )
            total, mixed = 0.0, 0.0
            for j, (ref, lo) in enumerate(parts):
                p = jnp.exp2(scores[j] - largest)
                total = total + jnp.sum(p, axis=-1, keepdims=True)
                mixed = mixed + dot_nt(p.astype(BF), ref[vrow, pl.ds(lo, 256)])
            qb[pl.ds(TOK * k, TOK), pl.ds(128 * i, 128)] = (mixed / total).astype(BF)
    drain("co")
    cross_mine, cross_other = qb[0:TOK, :], qb[TOK : 2 * TOK, :]

    def cross_out(i, carry):
        n = pl.ds(pl.multiple_of(256 * i, 256), 256)
        out[:, n] = (res[:, n] + outward(cross_mine, cross_other, CO0, i)).astype(BF)
        return carry

    lax.fori_loop(0, 6, cross_out, 0)
    assert used[0] <= NSEM
    for wait in started:
        wait()


def body(
    latent, modulation, cross_norm, norm_gains, w_main, text_states, w_text, tile_offsets, text_mask
):
    vmem = pl.BlockSpec(memory_space=pltpu.VMEM)
    smem = pl.BlockSpec(memory_space=pltpu.SMEM)
    hbm = pl.BlockSpec(memory_space=pl.ANY)
    result = pl.pallas_call(
        kernel,
        out_shape=jax.ShapeDtypeStruct((TOK, D), BF),
        in_specs=[hbm, vmem, vmem, vmem, hbm, hbm, hbm, smem, vmem],
        out_specs=vmem,
        scratch_shapes=[
            pltpu.VMEM((TOK, D), BF),
            pltpu.VMEM((48, 4608), BF),
            pltpu.VMEM((512, D), BF),
            pltpu.VMEM((48, D), BF),
            pltpu.VMEM((D, END), BF),
            pltpu.VMEM((D, END - SO0), BF),
            pltpu.VMEM((48, END), BF),
            pltpu.VMEM((3, 4 * TOK, D), BF),
            pltpu.VMEM((5, TOK, D), BF),
            pltpu.VMEM((3, 848, 768), BF),
            pltpu.VMEM((12 * TOK, HALF), F32),
            pltpu.VMEM((2, 12 * TOK, 128), F32),
            pltpu.VMEM((2 * TOK, HALF), F32),
            pltpu.VMEM((2, 2 * TOK, 128), F32),
            pltpu.VMEM((2 * TOK, HALF), BF),
            pltpu.VMEM((2, 32, WIN), F32),
            pltpu.VMEM((2, 3, TOK, WIN), F32),
            pltpu.VMEM((2 * TOK, HALF), BF),
            pltpu.VMEM((TOK, HALF), BF),
            pltpu.VMEM((TOK, D), F32),
            pltpu.VMEM((48, 512), BF),
            pltpu.SemaphoreType.DMA((NSEM,)),
            pltpu.SemaphoreType.DMA((NSEM,)),
            pltpu.SemaphoreType.DMA((4,)),
        ],
        compiler_params=pltpu.CompilerParams(
            collective_id=0, has_side_effects=True, vmem_limit_bytes=60 * 1024 * 1024
        ),
        cost_estimate=pl.CostEstimate(
            flops=6_000_000_000, bytes_accessed=6_000_000, transcendentals=3_000_000
        ),
    )(
        latent.reshape(TOK, D),
        modulation,
        cross_norm,
        norm_gains,
        w_main,
        text_states,
        w_text.T,
        tile_offsets,
        text_mask.reshape(1, 512),
    )
    return result.reshape(latent.shape)


def solution(mesh):
    placed = (
        P("tm", "height", None, None),
        P(),
        P(),
        P(),
        P("height", None),
        P(),
        P(None, "height"),
        P(None, "tm", "height", None, None),
        P(),
    )
    return jax.shard_map(
        body, mesh=mesh, in_specs=placed, out_specs=P("tm", "height", None, None), check_vma=False
    )
```
